32 devices in a mesh: groups: 1, ep: 32 (over z, y, x, core).
Axes of the slice: x: 2, y: 2, z: 4, core: 2. Of those that a mesh axis runs over, the one named last changes fastest.
Arguments:
- moe_rows: bfloat16 [1024, 7168], P(('groups', 'ep')), may hold values from -6 to 6
- routes: int32 [1024, 2], P(('groups', 'ep')), may hold values from 0 to 7, all different within a row; in each aligned block of 32 rows (0 to 31, 32 to 63, ...) at most 16 rows name the same one
- gate_weights: float32 [1024, 2], P(('groups', 'ep')), may hold values from 0.1 to 1
- gate_weight: bfloat16 [7168, 8192], P(None, 'ep'), may hold values from -0.0625 to 0.0625
- up_weight: bfloat16 [7168, 8192], P(None, 'ep'), may hold values from -0.0625 to 0.0625
- down_weight: bfloat16 [8192, 7168], P('ep'), may hold values from -0.1875 to 0.1875
- queries: bfloat16 [64, 128, 576], P(('groups', 'ep')), may hold values from -60 to 60
- latent_cache: bfloat16 [64, 256, 576], P(('groups', 'ep')), may hold values from -6 to 6
- lengths: int32 [64], P(('groups', 'ep')), may hold values from 2 to 256
Outputs:
- moe_out: bfloat16 [1024, 7168], P(('groups', 'ep'))
- attn_out: bfloat16 [64, 128, 512], P(('groups', 'ep'))
The draws below stay inside these ranges and needn't reach their ends.
Inputs may be any that keep to these rules, and one draw needn't show every extreme that they name: `routes`: each row names 2 different experts; within each device's block of 32 rows no expert is named more than 16 times, a bound that some block reaches.
All inputs are finite; a program needn't handle non-finite values.
Results may differ from the reference program's by a relative error of at most 0.008.
Values may be sent and summed in bfloat16 or wider, within the bound.
No kernel may reach another device: no remote copies, remote signals or barrier semaphores. Data moves between devices by JAX's collectives and lax.ppermute only.
A program may use at most 128 MiB of HBM per device.

```python
import math
import jax
import jax.numpy as jnp
import numpy as np
from jax import lax

D = 7168
FF = 1024
SPLIT = 4
FS = 256
TOPK = 2
EXPERTS = 8
ROWS_DEV = 32
CAP = 16
MOE_ROWS = 1024
HEADS = 128
NOPE = 512
ROPE = 64
CACHE_LEN = 256
ATT_ROWS = 64


def shared_cache(key):
    normal_part = jax.random.normal(jax.random.fold_in(key, 11), (ATT_ROWS, CACHE_LEN, NOPE + ROPE), jnp.float32)
    return normal_part


def draw_latent_cache(key, part):
    normal_part = shared_cache(key)
    values = jnp.clip(normal_part, -6.0, 6.0)
    return values.astype(jnp.bfloat16)


def draw_queries(key, part):
    key = jax.random.fold_in(key, 5)
    values = jnp.clip(jax.random.normal(key, (ATT_ROWS, HEADS, NOPE + ROPE), jnp.float32), -6.0, 6.0)
    return values.astype(jnp.bfloat16)


def draw_lengths(key, part):
    key = jax.random.fold_in(key, 7)
    values = jax.random.randint(key, (ATT_ROWS,), 2, CACHE_LEN + 1, dtype=jnp.int32)
    return values.at[0].set(CACHE_LEN).at[1].set(2)


def shard_levels(stream_key, extent, shards, smallest, top_value):
    level = 1.0
    for axis_at, shards_of in shards:
        draws = jax.random.uniform(jax.random.fold_in(jax.random.fold_in(stream_key, 6), axis_at), (shards_of,), jnp.float32, smallest / len(shards), top_value / len(shards))
        level = level * jnp.repeat(jnp.exp(draws), extent[axis_at] // shards_of).reshape((-1,) + (1,) * (len(extent) - 1 - axis_at))
    return level


def shared_out(rng, own, number, rows, number_of, top, most, skew):
    order = jax.random.permutation(rng, number_of)
    crowded, usual = load_shares(number_of, rows * top, most, skew, True), load_shares(number_of, rows * top, most, skew, False)
    places = jnp.arange(number_of)

    def named(tallies, offset_by):
        used = int((tallies > 0).sum())
        fixed = max(1, used // 4)
        shifted = fixed + (places - fixed + offset_by * (used - fixed)) % max(1, number_of - fixed)
        return jnp.zeros((number_of,), jnp.int32).at[order[jnp.where(places < fixed, places, shifted)]].set(jnp.asarray(tallies, jnp.int32))

    tallies = jnp.where(number % 4 == 0, named(crowded, number // 4), named(usual, number - number // 4 - 1))
    mixed = jax.random.permutation(jax.random.fold_in(own, 3), number_of)
    giver, taker = mixed[0:number_of // 2 * 2:2], mixed[1:number_of // 2 * 2:2]
    room = jnp.minimum(tallies[giver] - 1, most - tallies[taker]) // 2
    room = jnp.where((giver == order[0]) | (taker == order[0]) | (tallies[taker] == 0), 0, jnp.maximum(room, 0))
    shifted = jax.random.randint(jax.random.fold_in(own, 4), (number_of // 2,), 0, 1 << 20) % (room + 1)
    tallies = tallies.at[giver].add(-shifted).at[taker].add(shifted)
    members = jnp.searchsorted(jnp.cumsum(tallies), jnp.arange(rows * top), side="right").astype(jnp.int32)
    listing = members.reshape(top, rows).T
    listing = listing[jax.random.permutation(jax.random.fold_in(own, 1), rows)]
    offset_by = jax.random.randint(jax.random.fold_in(own, 2), (rows, 1), 0, top)
    return jnp.take_along_axis(listing, (jnp.arange(top)[None, :] + offset_by) % top, axis=1)


def load_shares(number_of, total, most, lean, full):
    weights = [(1 << 20) // math.isqrt(standing ** lean) + 1 for standing in range(1, number_of + 1)]
    largest = most if full else min(most, max(-(-total // number_of), total * weights[0] // sum(weights)))
    least = 1 if total - largest >= number_of - 1 else 0
    given, surplus = [largest] + [least] * (number_of - 1), total - largest - least * (number_of - 1)
    while surplus > 0:
        free = [i for i in range(1, number_of) if given[i] < largest] or [i for i in range(1, number_of) if given[i] < most]
        pool, remaining = sum([weights[i] for i in free]), surplus
        for i in free:
            addition = min(most - given[i], max(1, remaining * weights[i] // pool), surplus)
            given[i] = given[i] + addition
            surplus = surplus - addition
    return np.array(given)


def noise(own_key, dims, deviation, limit, pieces=(), kind=jnp.bfloat16):
    drawn = deviation * jax.random.normal(own_key, dims, jnp.float32)
    if pieces:
        drawn = drawn * shard_levels(own_key, dims, pieces, -0.22, 0.18)
    return jnp.clip(drawn, -limit, limit).astype(kind)


def setup_inputs(seed: int = 0, part: int = 0) -> dict:
    seeds = jax.random.split(jax.random.key(seed), 10)
    part_splits = jax.random.split(jax.random.fold_in(seeds[9], part), 10)
    moe_rows = noise(part_splits[0], (MOE_ROWS, D), 1.0, 6.0, ((0, 32),))
    routes_keys = jax.random.split(jax.random.fold_in(part_splits[1], 1), MOE_ROWS // ROWS_DEV)
    routes_turns = jax.random.permutation(jax.random.fold_in(part_splits[1], 3), MOE_ROWS // ROWS_DEV)
    routes = jax.vmap(lambda own, number: shared_out(jax.random.fold_in(part_splits[1], 2), own, number, ROWS_DEV, EXPERTS, TOPK, CAP, 2))(routes_keys, routes_turns).reshape((MOE_ROWS, TOPK))
    gate_weights = jnp.clip(jnp.exp(math.log(1.0) - 2.3025851 * jax.random.uniform(part_splits[2], (MOE_ROWS, TOPK), jnp.float32) ** shard_levels(part_splits[2], (MOE_ROWS, TOPK), ((0, 32),), -0.2, 0.2)), 0.1, 1.0)
    gate_weight = noise(seeds[3], (D, EXPERTS * FF), D ** -0.5, 0.0625, ((1, 32),))
    up_weight = noise(seeds[4], (D, EXPERTS * FF), D ** -0.5, 0.0625, ((1, 32),))
    down_weight = noise(seeds[5], (EXPERTS * FF, D), FF ** -0.5, 0.1875, ((0, 32),))
    queries = draw_queries(jax.random.fold_in(jax.random.fold_in(seeds[9], part), 71), part)
    latent_cache = draw_latent_cache(jax.random.fold_in(jax.random.fold_in(seeds[9], part), 71), part)
    lengths = draw_lengths(jax.random.fold_in(jax.random.fold_in(seeds[9], part), 71), part)
    return dict(moe_rows=moe_rows, routes=routes, gate_weights=gate_weights, gate_weight=gate_weight, up_weight=up_weight, down_weight=down_weight, queries=queries, latent_cache=latent_cache, lengths=lengths)


softmax_scale = 192.0 ** -0.5


def reference(moe_rows, routes, gate_weights, gate_weight, up_weight, down_weight, queries, latent_cache, lengths):
    def expert_term(running, expert):
        start = expert * FF
        gate_cols = lax.dynamic_slice_in_dim(gate_weight, start, FF, 1)
        up_cols = lax.dynamic_slice_in_dim(up_weight, start, FF, 1)
        down_rows = lax.dynamic_slice_in_dim(down_weight, start, FF, 0)
        gate_part = jnp.dot(moe_rows, gate_cols, preferred_element_type=jnp.float32)
        up_part = jnp.dot(moe_rows, up_cols, preferred_element_type=jnp.float32)
        hidden = (jax.nn.silu(gate_part) * up_part).astype(jnp.bfloat16)
        partial_out = jnp.einsum("tsf,sfd->tsd", hidden.reshape(MOE_ROWS, SPLIT, FS).astype(jnp.float32), down_rows.reshape(SPLIT, FS, D).astype(jnp.float32))
        partial_out = lax.optimization_barrier(partial_out.astype(jnp.bfloat16)).astype(jnp.float32)
        expert_out = jnp.sum(partial_out, axis=1)
        expert_out = lax.optimization_barrier(expert_out.astype(jnp.bfloat16)).astype(jnp.float32)
        chosen = jnp.sum(jnp.where(routes == expert, gate_weights, 0.0), axis=1)
        return running + chosen[:, None] * expert_out, None

    total, ignored = lax.scan(expert_term, jnp.zeros((MOE_ROWS, D), jnp.float32), jnp.arange(EXPERTS, dtype=jnp.int32))
    moe_out = total.astype(jnp.bfloat16)

    scores = jnp.einsum("rhc,rlc->rhl", queries.astype(jnp.float32), latent_cache.astype(jnp.float32)) * softmax_scale
    positions = jnp.arange(CACHE_LEN, dtype=jnp.int32)
    valid_mask = positions[None, None, :] < lengths[:, None, None]
    scores = jnp.where(valid_mask, scores, -1e30)
    highest = jnp.max(scores, axis=-1, keepdims=True)
    expons = jnp.where(valid_mask, jnp.exp(scores - highest), 0.0)
    weights = (expons / jnp.sum(expons, axis=-1, keepdims=True)).astype(jnp.bfloat16)
    attn_out = jnp.einsum("rhl,rlc->rhc", weights.astype(jnp.float32), latent_cache[:, :, :NOPE].astype(jnp.float32)).astype(jnp.bfloat16)
    return moe_out, attn_out
```

```python
import jax
import jax.numpy as jnp
from jax import lax
from jax.sharding import PartitionSpec as P

SPLIT = 4
NOPE = 512

softmax_scale = 192.0 ** (-0.5)


def attention(queries, latent_cache, lengths):
    scores = (
        jnp.einsum("rhc,rlc->rhl", queries, latent_cache, preferred_element_type=jnp.float32)
        * softmax_scale
    )
    positions = jnp.arange(latent_cache.shape[1], dtype=jnp.int32)
    valid_mask = positions[None, None, :] < lengths[:, None, None]
    scores = jnp.where(valid_mask, scores, -1e30)
    highest = jnp.max(scores, axis=-1, keepdims=True)
    expons = jnp.where(valid_mask, jnp.exp(scores - highest), 0.0)
    weights = (expons / jnp.sum(expons, axis=-1, keepdims=True)).astype(jnp.bfloat16)
    return jnp.einsum(
        "rhl,rlc->rhc", weights, latent_cache[:, :, :NOPE], preferred_element_type=jnp.float32
    ).astype(jnp.bfloat16)


def permutation(devices, far, near, swap_x, swap_core):
    outer_size = devices // 8
    pairs = []
    for source in range(devices):
        outer, inner, x, core = source // 8, source // 4 % 2, source // 2 % 2, source % 2
        target = ((outer + far) % outer_size * 2 + (inner ^ near)) * 4 + (x ^ swap_x) * 2 + (core ^ swap_core)
        pairs.append((source, target))
    return pairs


def body(
    moe_rows,
    routes,
    gate_weights,
    gate_weight,
    up_weight,
    down_weight,
    queries,
    latent_cache,
    lengths,
):
    devices = lax.axis_size("ep")
    experts = devices // SPLIT
    outer_size = experts // 2
    row_count, model_width = moe_rows.shape
    top_count = routes.shape[1]
    capacity = 2 * row_count * top_count * SPLIT // devices
    me = lax.axis_index("ep")
    outer, inner = me // 8, me // 4 % 2

    def send(array, far=0, near=0, swap_x=0, swap_core=0):
        return lax.ppermute(array, "ep", permutation(devices, far, near, swap_x, swap_core))

    gate_other, up_other, down_other = (
        send(w, swap_core=1) for w in (gate_weight, up_weight, down_weight)
    )

    flat_routes = routes.reshape(-1)
    relative = (flat_routes // 2 - outer + outer_size) % outer_size * 2 + ((flat_routes % 2) ^ inner)
    onehot = (relative[:, None] == jnp.arange(experts, dtype=jnp.int32)[None, :]).astype(jnp.int32)
    earlier = jnp.cumsum(onehot, axis=0) - onehot
    slot_ids = jnp.sum(earlier * onehot, axis=1)
    targets = (relative * capacity + slot_ids).reshape(row_count, top_count)
    placing = targets[:, :, None] == jnp.arange(experts * capacity, dtype=jnp.int32)[None, None, :]
    spread = jnp.any(placing, axis=1).astype(jnp.bfloat16)
    outgoing = jnp.einsum(
        "rp,rd->pd", spread, moe_rows, preferred_element_type=jnp.float32
    ).astype(jnp.bfloat16)

    order = [(far, near) for far in range(outer_size) for near in range(2)]
    blocks = {}
    crossed = {}
    for far, near in order:
        at = (far * 2 + near) * capacity
        block = outgoing[at : at + capacity]
        blocks[far, near] = block if (far, near) == (0, 0) else send(block, far, near)
    for key in order:
        crossed[key] = send(blocks[key], swap_x=1)

    def expert(rows):
        hidden = []
        for gate, up in ((gate_weight, up_weight), (gate_other, up_other)):
            gate_part = jnp.dot(rows, gate, preferred_element_type=jnp.float32)
            up_part = jnp.dot(rows, up, preferred_element_type=jnp.float32)
            hidden.append((jax.nn.silu(gate_part) * up_part).astype(jnp.bfloat16))
        return jnp.dot(hidden[0], down_weight, preferred_element_type=jnp.float32) + jnp.dot(
            hidden[1], down_other, preferred_element_type=jnp.float32
        )

    returned = {}
    for far in range(outer_size):
        keys = [(far, 0), (far, 1)]
        rows = jnp.concatenate([blocks[k] for k in keys] + [crossed[k] for k in keys], axis=0)
        partial = expert(rows)
        for i, key in enumerate(keys):
            mine = partial[i * capacity : (i + 1) * capacity]
            theirs = partial[(2 + i) * capacity : (3 + i) * capacity].astype(jnp.bfloat16)
            total = (mine + send(theirs, swap_x=1).astype(jnp.float32)).astype(jnp.bfloat16)
            returned[key] = total if key == (0, 0) else send(total, -key[0], key[1])
    combined = jnp.concatenate([returned[k] for k in order], axis=0)
    moe_out = 0.0
    for k in range(top_count):
        picked = jnp.dot(
            placing[:, k].astype(jnp.bfloat16), combined, preferred_element_type=jnp.float32
        )
        moe_out = moe_out + picked * gate_weights[:, k : k + 1]
    attn_out = attention(queries, latent_cache, lengths)
    return (moe_out.astype(jnp.bfloat16), attn_out)


def solution(mesh):
    in_specs = (
        P(("groups", "ep"), None),
        P(("groups", "ep"), None),
        P(("groups", "ep"), None),
        P(None, "ep"),
        P(None, "ep"),
        P("ep", None),
        P(("groups", "ep"), None, None),
        P(("groups", "ep"), None, None),
        P(("groups", "ep")),
    )
    out_specs = (P(("groups", "ep"), None), P(("groups", "ep"), None, None))
    return jax.shard_map(body, mesh=mesh, in_specs=in_specs, out_specs=out_specs, check_vma=False)
```

```python
import functools

import jax
import jax.numpy as jnp
from jax import lax
from jax.experimental import pallas as pl
from jax.experimental.pallas import tpu as pltpu
from jax.sharding import PartitionSpec as P

SPLIT = 4
NOPE = 512

softmax_scale = 192.0 ** (-0.5)


def attention(queries, latent_cache, lengths):
    scores = (
        jnp.einsum("rhc,rlc->rhl", queries, latent_cache, preferred_element_type=jnp.float32)
        * softmax_scale
    )
    positions = jnp.arange(latent_cache.shape[1], dtype=jnp.int32)
    valid_mask = positions[None, None, :] < lengths[:, None, None]
    scores = jnp.where(valid_mask, scores, -1e30)
    highest = jnp.max(scores, axis=-1, keepdims=True)
    expons = jnp.where(valid_mask, jnp.exp(scores - highest), 0.0)
    weights = (expons / jnp.sum(expons, axis=-1, keepdims=True)).astype(jnp.bfloat16)
    return jnp.einsum(
        "rhl,rlc->rhc", weights, latent_cache[:, :, :NOPE], preferred_element_type=jnp.float32
    ).astype(jnp.bfloat16)


def permutation(devices, far, near, swap_x, swap_core):
    outer_size = devices // 8
    pairs = []
    for source in range(devices):
        outer, inner, x, core = source // 8, source // 4 % 2, source // 2 % 2, source % 2
        target = ((outer + far) % outer_size * 2 + (inner ^ near)) * 4 + (x ^ swap_x) * 2 + (core ^ swap_core)
        pairs.append((source, target))
    return pairs


def after(array, *first):
    return lax.optimization_barrier((array,) + first)[0]


def chunk_of(width):
    return next(c for c in (1024, 512, 256, 128) if width % c == 0)


def expert_kernel(counts, steps, *refs):
    number = len(counts)
    blocks, (gate0, gate1, up0, up1, down0, down1) = refs[:number], refs[number : number + 6]
    outs = refs[number + 6 : 2 * number + 6]
    total, hidden = refs[2 * number + 6 :]
    step = pl.program_id(0)
    width = gate0.shape[1]

    @pl.when(step == 0)
    def _():
        total[...] = jnp.zeros_like(total)

    @pl.when(step < steps)
    def _():
        rows = jnp.concatenate([b[...] for b in blocks], axis=0)
        for i, w in enumerate((gate0, gate1, up0, up1)):
            total[:, i * width : (i + 1) * width] += jnp.dot(
                rows, w[...], preferred_element_type=jnp.float32
            )

    @pl.when(step == steps - 1)
    def _():
        gate, up = total[:, : 2 * width], total[:, 2 * width :]
        hidden[...] = (gate / (1.0 + jnp.exp(-gate)) * up).astype(jnp.bfloat16)

    @pl.when(step >= steps)
    def _():
        part = jnp.dot(hidden[:, :width], down0[...], preferred_element_type=jnp.float32)
        part += jnp.dot(hidden[:, width:], down1[...], preferred_element_type=jnp.float32)
        part = part.astype(jnp.bfloat16)
        at = 0
        for count, out in zip(counts, outs):
            out[...] = part[at : at + count]
            at += count


def expert(blocks, gates, ups, downs):
    counts = tuple(b.shape[0] for b in blocks)
    model_width, width = gates[0].shape
    chunk = chunk_of(model_width)
    steps = model_width // chunk
    slots = sum(counts)
    first = lambda i: jnp.minimum(i, steps - 1)
    second = lambda i: jnp.maximum(i - steps, 0)
    rows_in = [pl.BlockSpec((c, chunk), lambda i: (0, first(i))) for c in counts]
    rows_out = [pl.BlockSpec((c, chunk), lambda i: (0, second(i))) for c in counts]
    wide = pl.BlockSpec((chunk, width), lambda i: (first(i), 0))
    tall = pl.BlockSpec((width, chunk), lambda i: (0, second(i)))
    return pl.pallas_call(
        functools.partial(expert_kernel, counts, steps),
        grid=(2 * steps,),
        in_specs=rows_in + [wide] * 4 + [tall] * 2,
        out_specs=rows_out,
        out_shape=[jax.ShapeDtypeStruct((c, model_width), jnp.bfloat16) for c in counts],
        scratch_shapes=[
            pltpu.VMEM((slots, 4 * width), jnp.float32),
            pltpu.VMEM((slots, 2 * width), jnp.bfloat16),
        ],
        compiler_params=pltpu.CompilerParams(vmem_limit_bytes=56 * 1024 * 1024),
        cost_estimate=pl.CostEstimate(
            flops=12 * slots * model_width * width,
            bytes_accessed=12 * model_width * width + 4 * slots * model_width,
            transcendentals=2 * slots * width,
        ),
    )(*blocks, *gates, *ups, *downs)


def combine_kernel(number, *refs):
    blocks, (places, shares, out) = refs[:number], refs[number:]
    rows = jnp.concatenate([b[...] for b in blocks], axis=0)
    total = 0.0
    for k in range(shares.shape[1]):
        picked = jnp.dot(places[k], rows, preferred_element_type=jnp.float32)
        total = total + picked * shares[:, k : k + 1]
    out[...] = total.astype(out.dtype)


def combine(blocks, places, shares):
    number, (capacity, model_width) = len(blocks), blocks[0].shape
    row_count, top_count = shares.shape
    chunk = chunk_of(model_width)
    return pl.pallas_call(
        functools.partial(combine_kernel, number),
        grid=(model_width // chunk,),
        in_specs=[pl.BlockSpec((capacity, chunk), lambda i: (0, i))] * number
        + [
            pl.BlockSpec((top_count, row_count, number * capacity), lambda i: (0, 0, 0)),
            pl.BlockSpec((row_count, top_count), lambda i: (0, 0)),
        ],
        out_specs=pl.BlockSpec((row_count, chunk), lambda i: (0, i)),
        out_shape=jax.ShapeDtypeStruct((row_count, model_width), jnp.bfloat16),
    )(*blocks, places, shares)


def body(
    moe_rows,
    routes,
    gate_weights,
    gate_weight,
    up_weight,
    down_weight,
    queries,
    latent_cache,
    lengths,
):
    devices = lax.axis_size("ep")
    experts = devices // SPLIT
    outer_size = experts // 2
    row_count, model_width = moe_rows.shape
    top_count = routes.shape[1]
    capacity = 2 * row_count * top_count * SPLIT // devices
    me = lax.axis_index("ep")
    outer, inner = me // 8, me // 4 % 2

    def send(array, far=0, near=0, swap_x=0, swap_core=0):
        return lax.ppermute(array, "ep", permutation(devices, far, near, swap_x, swap_core))

    flat_routes = routes.reshape(-1)
    relative = (flat_routes // 2 - outer + outer_size) % outer_size * 2 + ((flat_routes % 2) ^ inner)
    onehot = (relative[:, None] == jnp.arange(experts, dtype=jnp.int32)[None, :]).astype(jnp.int32)
    earlier = jnp.cumsum(onehot, axis=0) - onehot
    slot_ids = jnp.sum(earlier * onehot, axis=1)
    targets = (relative * capacity + slot_ids).reshape(row_count, top_count)
    placing = targets[:, :, None] == jnp.arange(experts * capacity, dtype=jnp.int32)[None, None, :]
    spread = jnp.any(placing, axis=1).astype(jnp.bfloat16)
    outgoing = jnp.einsum(
        "rp,rd->pd", spread, moe_rows, preferred_element_type=jnp.float32
    ).astype(jnp.bfloat16)
    places = placing.astype(jnp.bfloat16).transpose(1, 0, 2)

    def outgoing_block(far, near):
        at = (far * 2 + near) * capacity
        return outgoing[at : at + capacity]

    close = sorted({1, outer_size - 1} - {0})
    rest = [f for f in range(2, outer_size - 1)]
    rows, crossed = {(0, 0): outgoing_block(0, 0)}, {}

    def step(key, *first):
        rows[key] = send(after(outgoing_block(*key), *first), *key)

    def cross(f, *first):
        crossed[f] = send(
            after(jnp.concatenate([rows[f, 0], rows[f, 1]], axis=0), *first), swap_x=1
        )

    step((0, 1))
    for f in close:
        step((f, 0))
    gate_other = send(after(gate_weight, outgoing), swap_core=1)
    begun = [gate_other, rows[0, 1]] + [rows[f, 0] for f in close]
    up_other = send(after(up_weight, *begun), swap_core=1)
    cross(0, *begun)
    for f in close:
        step((f, 1), *begun)
    begun = [up_other, crossed[0]] + [rows[f, 1] for f in close]
    down_other = send(after(down_weight, *begun), swap_core=1)
    for f in close:
        cross(f, *begun)
    for f in rest:
        for n in range(2):
            step((f, n), *begun)
    for f in rest:
        cross(f, down_other)

    mine, theirs = {}, {}

    def run(fars):
        blocks = [rows[f, n] for f in fars for n in range(2)] + [crossed[f] for f in fars]
        outs = expert(
            blocks, (gate_weight, gate_other), (up_weight, up_other), (down_weight, down_other)
        )
        for i, f in enumerate(fars):
            mine[f, 0], mine[f, 1] = outs[2 * i : 2 * i + 2]
            theirs[f] = outs[2 * len(fars) + i]

    run([0] + close)
    back, returned = {}, {}

    def finish(f, *first):
        came = after(back[f], *first)
        for n in range(2):
            part = came[n * capacity : (n + 1) * capacity]
            total = (mine[f, n].astype(jnp.float32) + part.astype(jnp.float32)).astype(jnp.bfloat16)
            returned[f, n] = total if (f, n) == (0, 0) else send(total, -f, n)

    for f in close:
        back[f] = send(theirs[f], swap_x=1)
    run(rest)
    for f in rest:
        back[f] = send(theirs[f], swap_x=1)
    back[0] = send(after(theirs[0], back[close[-1]]), swap_x=1)
    for f in close + rest:
        finish(f)
    finish(0, returned[rest[-1], 0])
    moe_out = combine(
        [returned[f, n] for f in range(outer_size) for n in range(2)], places, gate_weights
    )
    attn_out = attention(queries, latent_cache, lengths)
    return (moe_out, attn_out)


def solution(mesh):
    in_specs = (
        P(("groups", "ep"), None),
        P(("groups", "ep"), None),
        P(("groups", "ep"), None),
        P(None, "ep"),
        P(None, "ep"),
        P("ep", None),
        P(("groups", "ep"), None, None),
        P(("groups", "ep"), None, None),
        P(("groups", "ep")),
    )
    out_specs = (P(("groups", "ep"), None), P(("groups", "ep"), None, None))
    return jax.shard_map(body, mesh=mesh, in_specs=in_specs, out_specs=out_specs, check_vma=False)
```

```python
import functools

import jax
import jax.numpy as jnp
from jax import lax
from jax.experimental import pallas as pl
from jax.experimental.pallas import tpu as pltpu
from jax.sharding import PartitionSpec as P

SPLIT = 4
NOPE = 512

softmax_scale = 192.0 ** (-0.5)


def attention(queries, latent_cache, lengths):
    scores = (
        jnp.einsum("rhc,rlc->rhl", queries, latent_cache, preferred_element_type=jnp.float32)
        * softmax_scale
    )
    positions = jnp.arange(latent_cache.shape[1], dtype=jnp.int32)
    valid_mask = positions[None, None, :] < lengths[:, None, None]
    scores = jnp.where(valid_mask, scores, -1e30)
    highest = jnp.max(scores, axis=-1, keepdims=True)
    expons = jnp.where(valid_mask, jnp.exp(scores - highest), 0.0)
    weights = (expons / jnp.sum(expons, axis=-1, keepdims=True)).astype(jnp.bfloat16)
    return jnp.einsum(
        "rhl,rlc->rhc", weights, latent_cache[:, :, :NOPE], preferred_element_type=jnp.float32
    ).astype(jnp.bfloat16)


def permutation(devices, far, near, swap_x, swap_core):
    outer_size = devices // 8
    pairs = []
    for source in range(devices):
        outer, inner, x, core = source // 8, source // 4 % 2, source // 2 % 2, source % 2
        target = ((outer + far) % outer_size * 2 + (inner ^ near)) * 4 + (x ^ swap_x) * 2 + (core ^ swap_core)
        pairs.append((source, target))
    return pairs


def after(array, *first):
    return lax.optimization_barrier((array,) + first)[0]


def expert_kernel(counts, parts, *refs):
    number = len(counts)
    blocks, weights, outs = refs[:number], refs[number : number + 6], refs[number + 6 : 2 * number + 6]
    wide, tall, total, hidden, arrived = refs[2 * number + 6 :]
    model_width, width = weights[0].shape
    part_width = model_width // parts
    spans = [slice(p * part_width, (p + 1) * part_width) for p in range(parts)]
    wide_copies = [
        [
            pltpu.make_async_copy(weights[i].at[span], wide.at[i, span], arrived.at[p * 6 + i])
            for i in range(4)
        ]
        for p, span in enumerate(spans)
    ]
    tall_copies = [
        [
            pltpu.make_async_copy(
                weights[4 + i].at[:, span], tall.at[i, :, span], arrived.at[p * 6 + 4 + i]
            )
            for i in range(2)
        ]
        for p, span in enumerate(spans)
    ]
    for copies in wide_copies + tall_copies:
        for copy in copies:
            copy.start()
    for p, span in enumerate(spans):
        rows = jnp.concatenate([b[:, span] for b in blocks], axis=0)
        for i in range(4):
            wide_copies[p][i].wait()
            product = jnp.dot(rows, wide[i, span], preferred_element_type=jnp.float32)
            columns = slice(i * width, (i + 1) * width)
            total[:, columns] = product if p == 0 else total[:, columns] + product
    gate, up = total[:, : 2 * width], total[:, 2 * width :]
    hidden[...] = (gate / (1.0 + jnp.exp(-gate)) * up).astype(jnp.bfloat16)
    piece = part_width // 4
    for p in range(parts):
        for copy in tall_copies[p]:
            copy.wait()
        for q in range(4):
            columns = slice(p * part_width + q * piece, p * part_width + (q + 1) * piece)
            part = jnp.dot(
                hidden[:, :width], tall[0, :, columns], preferred_element_type=jnp.float32
            )
            part += jnp.dot(
                hidden[:, width:], tall[1, :, columns], preferred_element_type=jnp.float32
            )
            part = part.astype(jnp.bfloat16)
            at = 0
            for count, out in zip(counts, outs):
                out[:, columns] = part[at : at + count]
                at += count


def expert(blocks, gates, ups, downs):
    counts = tuple(b.shape[0] for b in blocks)
    model_width, width = gates[0].shape
    slots, parts = sum(counts), 2
    return pl.pallas_call(
        functools.partial(expert_kernel, counts, parts),
        in_specs=[pl.BlockSpec(memory_space=pltpu.VMEM)] * len(counts)
        + [pl.BlockSpec(memory_space=pl.ANY)] * 6,
        out_specs=[pl.BlockSpec(memory_space=pltpu.VMEM)] * len(counts),
        out_shape=[jax.ShapeDtypeStruct((c, model_width), jnp.bfloat16) for c in counts],
        scratch_shapes=[
            pltpu.VMEM((4, model_width, width), jnp.bfloat16),
            pltpu.VMEM((2, width, model_width), jnp.bfloat16),
            pltpu.VMEM((slots, 4 * width), jnp.float32),
            pltpu.VMEM((slots, 2 * width), jnp.bfloat16),
            pltpu.SemaphoreType.DMA((6 * parts,)),
        ],
        compiler_params=pltpu.CompilerParams(vmem_limit_bytes=60 * 1024 * 1024),
        cost_estimate=pl.CostEstimate(
            flops=12 * slots * model_width * width,
            bytes_accessed=12 * model_width * width + 4 * slots * model_width,
            transcendentals=2 * slots * width,
        ),
    )(*blocks, *gates, *ups, *downs)


def combine_kernel(number, *refs):
    blocks, (places, shares, out) = refs[:number], refs[number:]
    model_width = out.shape[1]
    piece = model_width // 7
    for lo in range(0, model_width, piece):
        columns = slice(lo, lo + piece)
        rows = jnp.concatenate([b[:, columns] for b in blocks], axis=0)
        total = 0.0
        for k in range(shares.shape[1]):
            picked = jnp.dot(places[k], rows, preferred_element_type=jnp.float32)
            total = total + picked * shares[:, k : k + 1]
        out[:, columns] = total.astype(out.dtype)


def combine(blocks, places, shares):
    return pl.pallas_call(
        functools.partial(combine_kernel, len(blocks)),
        out_shape=jax.ShapeDtypeStruct((shares.shape[0], blocks[0].shape[1]), jnp.bfloat16),
    )(*blocks, places, shares)


def body(
    moe_rows,
    routes,
    gate_weights,
    gate_weight,
    up_weight,
    down_weight,
    queries,
    latent_cache,
    lengths,
):
    devices = lax.axis_size("ep")
    experts = devices // SPLIT
    outer_size = experts // 2
    row_count, model_width = moe_rows.shape
    top_count = routes.shape[1]
    capacity = 2 * row_count * top_count * SPLIT // devices
    me = lax.axis_index("ep")
    outer, inner = me // 8, me // 4 % 2

    def send(array, far=0, near=0, swap_x=0, swap_core=0):
        return lax.ppermute(array, "ep", permutation(devices, far, near, swap_x, swap_core))

    flat_routes = routes.reshape(-1)
    relative = (flat_routes // 2 - outer + outer_size) % outer_size * 2 + ((flat_routes % 2) ^ inner)
    onehot = (relative[:, None] == jnp.arange(experts, dtype=jnp.int32)[None, :]).astype(jnp.int32)
    earlier = jnp.cumsum(onehot, axis=0) - onehot
    slot_ids = jnp.sum(earlier * onehot, axis=1)
    targets = (relative * capacity + slot_ids).reshape(row_count, top_count)
    placing = targets[:, :, None] == jnp.arange(experts * capacity, dtype=jnp.int32)[None, None, :]
    spread = jnp.any(placing, axis=1).astype(jnp.bfloat16)
    outgoing = jnp.einsum(
        "rp,rd->pd", spread, moe_rows, preferred_element_type=jnp.float32
    ).astype(jnp.bfloat16)
    places = placing.astype(jnp.bfloat16).transpose(1, 0, 2)

    def outgoing_block(far, near):
        at = (far * 2 + near) * capacity
        return outgoing[at : at + capacity]

    close = sorted({1, outer_size - 1} - {0})
    rest = [f for f in range(2, outer_size - 1)]
    rows, crossed = {(0, 0): outgoing_block(0, 0)}, {}

    def step(key, *first):
        rows[key] = send(after(outgoing_block(*key), *first), *key)

    def cross(f, *first):
        crossed[f] = send(
            after(jnp.concatenate([rows[f, 0], rows[f, 1]], axis=0), *first), swap_x=1
        )

    gate_other = send(gate_weight, swap_core=1)
    step((0, 1))
    for f in rest:
        for n in range(2):
            step((f, n))
    step((close[0], 0), rows[0, 1])
    up_other = send(after(up_weight, gate_other, rows[0, 1], rows[rest[0], 0]), swap_core=1)
    cross(0)
    begun = [up_other, crossed[0], rows[rest[-1], 1], rows[close[0], 0]]
    down_other = send(after(down_weight, *begun), swap_core=1)
    step((close[0], 1), rows[rest[0], 0])
    step((close[1], 0), rows[rest[0], 1])
    step((close[1], 1), rows[rest[-1], 1])
    for f in rest:
        cross(f, crossed[0])
    for f in close:
        cross(f, *(crossed[r] for r in rest))

    mine, theirs = {}, {}

    def run(fars):
        blocks = [rows[f, n] for f in fars for n in range(2)] + [crossed[f] for f in fars]
        outs = expert(
            blocks, (gate_weight, gate_other), (up_weight, up_other), (down_weight, down_other)
        )
        for i, f in enumerate(fars):
            mine[f, 0], mine[f, 1] = outs[2 * i : 2 * i + 2]
            theirs[f] = outs[2 * len(fars) + i]

    back, returned = {}, {}

    def finish(f, *first):
        came = after(back[f], *first)
        for n in range(2):
            part = came[n * capacity : (n + 1) * capacity]
            total = (mine[f, n].astype(jnp.float32) + part.astype(jnp.float32)).astype(jnp.bfloat16)
            returned[f, n] = total if (f, n) == (0, 0) else send(total, -f, n)

    run([0] + rest)
    for f in rest:
        back[f] = send(theirs[f], swap_x=1)
    run(close)
    for f in close:
        back[f] = send(theirs[f], swap_x=1)
    back[0] = send(after(theirs[0], back[close[0]]), swap_x=1)
    for f in rest + close:
        finish(f)
    finish(0, returned[close[-1], 0])
    moe_out = combine(
        [returned[f, n] for f in range(outer_size) for n in range(2)], places, gate_weights
    )
    attn_out = attention(queries, latent_cache, lengths)
    return (moe_out, attn_out)


def solution(mesh):
    in_specs = (
        P(("groups", "ep"), None),
        P(("groups", "ep"), None),
        P(("groups", "ep"), None),
        P(None, "ep"),
        P(None, "ep"),
        P("ep", None),
        P(("groups", "ep"), None, None),
        P(("groups", "ep"), None, None),
        P(("groups", "ep")),
    )
    out_specs = (P(("groups", "ep"), None), P(("groups", "ep"), None, None))
    return jax.shard_map(body, mesh=mesh, in_specs=in_specs, out_specs=out_specs, check_vma=False)
```

```python
import functools

import jax
import jax.numpy as jnp
from jax import lax
from jax.experimental import pallas as pl
from jax.experimental.pallas import tpu as pltpu
from jax.sharding import PartitionSpec as P

SPLIT = 4
NOPE = 512

softmax_scale = 192.0 ** (-0.5)


def attention(queries, latent_cache, lengths):
    scores = (
        jnp.einsum("rhc,rlc->rhl", queries, latent_cache, preferred_element_type=jnp.float32)
        * softmax_scale
    )
    positions = jnp.arange(latent_cache.shape[1], dtype=jnp.int32)
    valid_mask = positions[None, None, :] < lengths[:, None, None]
    scores = jnp.where(valid_mask, scores, -1e30)
    highest = jnp.max(scores, axis=-1, keepdims=True)
    expons = jnp.where(valid_mask, jnp.exp(scores - highest), 0.0)
    weights = (expons / jnp.sum(expons, axis=-1, keepdims=True)).astype(jnp.bfloat16)
    return jnp.einsum(
        "rhl,rlc->rhc", weights, latent_cache[:, :, :NOPE], preferred_element_type=jnp.float32
    ).astype(jnp.bfloat16)


def permutation(devices, far, near, swap_x, swap_core):
    outer_size = devices // 8
    pairs = []
    for source in range(devices):
        outer, inner, x, core = source // 8, source // 4 % 2, source // 2 % 2, source % 2
        target = ((outer + far) % outer_size * 2 + (inner ^ near)) * 4 + (x ^ swap_x) * 2 + (core ^ swap_core)
        pairs.append((source, target))
    return pairs


def after(array, *first):
    return lax.optimization_barrier((array,) + first)[0]


def expert_kernel(counts, parts, *refs):
    number = len(counts)
    blocks, weights, outs = refs[:number], refs[number : number + 6], refs[number + 6 : 2 * number + 6]
    wide, tall, total, hidden, arrived = refs[2 * number + 6 :]
    model_width, width = weights[0].shape
    part_width = model_width // parts
    spans = [slice(p * part_width, (p + 1) * part_width) for p in range(parts)]
    wide_copies = [
        [
            pltpu.make_async_copy(weights[i].at[span], wide.at[i, span], arrived.at[p * 6 + i])
            for i in range(4)
        ]
        for p, span in enumerate(spans)
    ]
    tall_copies = [
        [
            pltpu.make_async_copy(
                weights[4 + i].at[:, span], tall.at[i, :, span], arrived.at[p * 6 + 4 + i]
            )
            for i in range(2)
        ]
        for p, span in enumerate(spans)
    ]
    for copies in wide_copies + tall_copies:
        for copy in copies:
            copy.start()
    for p, span in enumerate(spans):
        rows = jnp.concatenate([b[:, span] for b in blocks], axis=0)
        for i in range(4):
            wide_copies[p][i].wait()
            product = jnp.dot(rows, wide[i, span], preferred_element_type=jnp.float32)
            columns = slice(i * width, (i + 1) * width)
            total[:, columns] = product if p == 0 else total[:, columns] + product
    gate, up = total[:, : 2 * width], total[:, 2 * width :]
    hidden[...] = (gate / (1.0 + jnp.exp(-gate)) * up).astype(jnp.bfloat16)
    piece = part_width // 4
    for p in range(parts):
        for copy in tall_copies[p]:
            copy.wait()
        for q in range(4):
            columns = slice(p * part_width + q * piece, p * part_width + (q + 1) * piece)
            part = jnp.dot(
                hidden[:, :width], tall[0, :, columns], preferred_element_type=jnp.float32
            )
            part += jnp.dot(
                hidden[:, width:], tall[1, :, columns], preferred_element_type=jnp.float32
            )
            part = part.astype(jnp.bfloat16)
            at = 0
            for count, out in zip(counts, outs):
                out[:, columns] = part[at : at + count]
                at += count


def expert(blocks, gates, ups, downs):
    counts = tuple(b.shape[0] for b in blocks)
    model_width, width = gates[0].shape
    slots, parts = sum(counts), 2
    return pl.pallas_call(
        functools.partial(expert_kernel, counts, parts),
        in_specs=[pl.BlockSpec(memory_space=pltpu.VMEM)] * len(counts)
        + [pl.BlockSpec(memory_space=pl.ANY)] * 6,
        out_specs=[pl.BlockSpec(memory_space=pltpu.VMEM)] * len(counts),
        out_shape=[jax.ShapeDtypeStruct((c, model_width), jnp.bfloat16) for c in counts],
        scratch_shapes=[
            pltpu.VMEM((4, model_width, width), jnp.bfloat16),
            pltpu.VMEM((2, width, model_width), jnp.bfloat16),
            pltpu.VMEM((slots, 4 * width), jnp.float32),
            pltpu.VMEM((slots, 2 * width), jnp.bfloat16),
            pltpu.SemaphoreType.DMA((6 * parts,)),
        ],
        compiler_params=pltpu.CompilerParams(vmem_limit_bytes=60 * 1024 * 1024),
        cost_estimate=pl.CostEstimate(
            flops=12 * slots * model_width * width,
            bytes_accessed=12 * model_width * width + 4 * slots * model_width,
            transcendentals=2 * slots * width,
        ),
    )(*blocks, *gates, *ups, *downs)


def combine_kernel(number, *refs):
    blocks, (places, shares, out) = refs[:number], refs[number:]
    model_width = out.shape[1]
    piece = model_width // 7
    for lo in range(0, model_width, piece):
        columns = slice(lo, lo + piece)
        rows = jnp.concatenate([b[:, columns] for b in blocks], axis=0)
        total = 0.0
        for k in range(shares.shape[1]):
            picked = jnp.dot(places[k], rows, preferred_element_type=jnp.float32)
            total = total + picked * shares[:, k : k + 1]
        out[:, columns] = total.astype(out.dtype)


def combine(blocks, places, shares):
    return pl.pallas_call(
        functools.partial(combine_kernel, len(blocks)),
        out_shape=jax.ShapeDtypeStruct((shares.shape[0], blocks[0].shape[1]), jnp.bfloat16),
    )(*blocks, places, shares)


def body(
    moe_rows,
    routes,
    gate_weights,
    gate_weight,
    up_weight,
    down_weight,
    queries,
    latent_cache,
    lengths,
):
    devices = lax.axis_size("ep")
    experts = devices // SPLIT
    outer_size = experts // 2
    row_count, model_width = moe_rows.shape
    top_count = routes.shape[1]
    capacity = 2 * row_count * top_count * SPLIT // devices
    me = lax.axis_index("ep")
    outer, inner = me // 8, me // 4 % 2

    def send(array, far=0, near=0, swap_x=0, swap_core=0):
        return lax.ppermute(array, "ep", permutation(devices, far, near, swap_x, swap_core))

    flat_routes = routes.reshape(-1)
    relative = (flat_routes // 2 - outer + outer_size) % outer_size * 2 + ((flat_routes % 2) ^ inner)
    onehot = (relative[:, None] == jnp.arange(experts, dtype=jnp.int32)[None, :]).astype(jnp.int32)
    earlier = jnp.cumsum(onehot, axis=0) - onehot
    slot_ids = jnp.sum(earlier * onehot, axis=1)
    targets = (relative * capacity + slot_ids).reshape(row_count, top_count)
    placing = targets[:, :, None] == jnp.arange(experts * capacity, dtype=jnp.int32)[None, None, :]
    spread = jnp.any(placing, axis=1).astype(jnp.bfloat16)
    outgoing = jnp.einsum(
        "rp,rd->pd", spread, moe_rows, preferred_element_type=jnp.float32
    ).astype(jnp.bfloat16)
    places = placing.astype(jnp.bfloat16).transpose(1, 0, 2)

    def outgoing_block(far, near):
        at = (far * 2 + near) * capacity
        return outgoing[at : at + capacity]

    close = sorted({1, outer_size - 1} - {0})
    rest = [(f, n) for f in range(2, outer_size - 1) for n in range(2)]
    own, near = [(0, 0)], [(0, 1)] + [(close[0], n) for n in range(2)]
    last = [(close[1], n) for n in range(2)]
    rows, crossed = {(0, 0): outgoing_block(0, 0)}, {}

    def step(key, *first):
        rows[key] = send(after(outgoing_block(*key), *first), *key)

    def cross(keys, *first):
        together = jnp.concatenate([rows[key] for key in keys], axis=0)
        crossed[keys[0]] = send(after(together, *first) if first else together, swap_x=1)

    gate_other = send(gate_weight, swap_core=1)
    up_other = send(up_weight, swap_core=1)
    for key in rest:
        step(key)
    cross(own)
    begun = [gate_other, up_other, crossed[0, 0]] + [rows[key] for key in rest]
    cross(rest, *begun)
    for key in near:
        step(key, *begun)
    begun = [crossed[rest[0]]] + [rows[key] for key in near]
    down_other = send(after(down_weight, *begun), swap_core=1)
    for key in last:
        step(key, *begun)
    cross(near, *begun)
    cross(last, crossed[near[0]], down_other)

    mine, theirs = {}, {}

    def run(*groups):
        keys = [key for group in groups for key in group]
        blocks = [rows[key] for key in keys] + [crossed[group[0]] for group in groups]
        outs = expert(
            blocks, (gate_weight, gate_other), (up_weight, up_other), (down_weight, down_other)
        )
        mine.update(zip(keys, outs))
        theirs.update(zip([group[0] for group in groups], outs[len(keys) :]))

    back, returned = {}, {}

    def finish(keys, *first):
        came = after(back[keys[0]], *first)
        for i, key in enumerate(keys):
            part = came[i * capacity : (i + 1) * capacity]
            total = (mine[key].astype(jnp.float32) + part.astype(jnp.float32)).astype(jnp.bfloat16)
            returned[key] = total if key == (0, 0) else send(total, -key[0], key[1])

    run(own, rest)
    back[rest[0]] = send(theirs[rest[0]], swap_x=1)
    run(near, last)
    for group in (near, last):
        back[group[0]] = send(theirs[group[0]], swap_x=1)
    back[own[0]] = send(after(theirs[own[0]], back[near[0]]), swap_x=1)
    for group in (rest, near, last):
        finish(group)
    finish(own, returned[near[1]])
    moe_out = combine(
        [returned[f, n] for f in range(outer_size) for n in range(2)], places, gate_weights
    )
    attn_out = attention(queries, latent_cache, lengths)
    return (moe_out, attn_out)


def solution(mesh):
    in_specs = (
        P(("groups", "ep"), None),
        P(("groups", "ep"), None),
        P(("groups", "ep"), None),
        P(None, "ep"),
        P(None, "ep"),
        P("ep", None),
        P(("groups", "ep"), None, None),
        P(("groups", "ep"), None, None),
        P(("groups", "ep")),
    )
    out_specs = (P(("groups", "ep"), None), P(("groups", "ep"), None, None))
    return jax.shard_map(body, mesh=mesh, in_specs=in_specs, out_specs=out_specs, check_vma=False)
```

```python
import functools

import jax
import jax.numpy as jnp
from jax import lax
from jax.experimental import pallas as pl
from jax.experimental.pallas import tpu as pltpu
from jax.sharding import PartitionSpec as P

SPLIT = 4
NOPE = 512

softmax_scale = 192.0 ** (-0.5)


def attention(queries, latent_cache, lengths):
    scores = (
        jnp.einsum("rhc,rlc->rhl", queries, latent_cache, preferred_element_type=jnp.float32)
        * softmax_scale
    )
    positions = jnp.arange(latent_cache.shape[1], dtype=jnp.int32)
    valid_mask = positions[None, None, :] < lengths[:, None, None]
    scores = jnp.where(valid_mask, scores, -1e30)
    highest = jnp.max(scores, axis=-1, keepdims=True)
    expons = jnp.where(valid_mask, jnp.exp(scores - highest), 0.0)
    weights = (expons / jnp.sum(expons, axis=-1, keepdims=True)).astype(jnp.bfloat16)
    return jnp.einsum(
        "rhl,rlc->rhc", weights, latent_cache[:, :, :NOPE], preferred_element_type=jnp.float32
    ).astype(jnp.bfloat16)


def permutation(devices, far, near, swap_x, swap_core):
    outer_size = devices // 8
    pairs = []
    for source in range(devices):
        outer, inner, x, core = source // 8, source // 4 % 2, source // 2 % 2, source % 2
        target = ((outer + far) % outer_size * 2 + (inner ^ near)) * 4 + (x ^ swap_x) * 2 + (core ^ swap_core)
        pairs.append((source, target))
    return pairs


def after(array, *first):
    return lax.optimization_barrier((array,) + first)[0]


def expert_kernel(counts, parts, *refs):
    number = len(counts)
    blocks, weights, outs = refs[:number], refs[number : number + 6], refs[number + 6 : 2 * number + 6]
    wide, tall, total, hidden, arrived = refs[2 * number + 6 :]
    model_width, width = weights[0].shape
    part_width = model_width // parts
    spans = [slice(p * part_width, (p + 1) * part_width) for p in range(parts)]
    wide_copies = [
        [
            pltpu.make_async_copy(weights[i].at[span], wide.at[i, span], arrived.at[p * 6 + i])
            for i in range(4)
        ]
        for p, span in enumerate(spans)
    ]
    tall_copies = [
        [
            pltpu.make_async_copy(
                weights[4 + i].at[:, span], tall.at[i, :, span], arrived.at[p * 6 + 4 + i]
            )
            for i in range(2)
        ]
        for p, span in enumerate(spans)
    ]
    for copies in wide_copies + tall_copies:
        for copy in copies:
            copy.start()
    for p, span in enumerate(spans):
        rows = jnp.concatenate([b[:, span] for b in blocks], axis=0)
        for i in range(4):
            wide_copies[p][i].wait()
            product = jnp.dot(rows, wide[i, span], preferred_element_type=jnp.float32)
            columns = slice(i * width, (i + 1) * width)
            total[:, columns] = product if p == 0 else total[:, columns] + product
    gate, up = total[:, : 2 * width], total[:, 2 * width :]
    hidden[...] = (gate / (1.0 + jnp.exp(-gate)) * up).astype(jnp.bfloat16)
    piece = part_width // 4
    for p in range(parts):
        for copy in tall_copies[p]:
            copy.wait()
        for q in range(4):
            columns = slice(p * part_width + q * piece, p * part_width + (q + 1) * piece)
            part = jnp.dot(
                hidden[:, :width], tall[0, :, columns], preferred_element_type=jnp.float32
            )
            part += jnp.dot(
                hidden[:, width:], tall[1, :, columns], preferred_element_type=jnp.float32
            )
            part = part.astype(jnp.bfloat16)
            at = 0
            for count, out in zip(counts, outs):
                out[:, columns] = part[at : at + count]
                at += count


def expert(blocks, gates, ups, downs):
    counts = tuple(b.shape[0] for b in blocks)
    model_width, width = gates[0].shape
    slots, parts = sum(counts), 2
    return pl.pallas_call(
        functools.partial(expert_kernel, counts, parts),
        in_specs=[pl.BlockSpec(memory_space=pltpu.VMEM)] * len(counts)
        + [pl.BlockSpec(memory_space=pl.ANY)] * 6,
        out_specs=[pl.BlockSpec(memory_space=pltpu.VMEM)] * len(counts),
        out_shape=[jax.ShapeDtypeStruct((c, model_width), jnp.bfloat16) for c in counts],
        scratch_shapes=[
            pltpu.VMEM((4, model_width, width), jnp.bfloat16),
            pltpu.VMEM((2, width, model_width), jnp.bfloat16),
            pltpu.VMEM((slots, 4 * width), jnp.float32),
            pltpu.VMEM((slots, 2 * width), jnp.bfloat16),
            pltpu.SemaphoreType.DMA((6 * parts,)),
        ],
        compiler_params=pltpu.CompilerParams(vmem_limit_bytes=60 * 1024 * 1024),
        cost_estimate=pl.CostEstimate(
            flops=12 * slots * model_width * width,
            bytes_accessed=12 * model_width * width + 4 * slots * model_width,
            transcendentals=2 * slots * width,
        ),
    )(*blocks, *gates, *ups, *downs)


def combine_kernel(number, *refs):
    blocks, (places, shares, out) = refs[:number], refs[number:]
    model_width = out.shape[1]
    piece = model_width // 7
    for lo in range(0, model_width, piece):
        columns = slice(lo, lo + piece)
        rows = jnp.concatenate([b[:, columns] for b in blocks], axis=0)
        total = 0.0
        for k in range(shares.shape[1]):
            picked = jnp.dot(places[k], rows, preferred_element_type=jnp.float32)
            total = total + picked * shares[:, k : k + 1]
        out[:, columns] = total.astype(out.dtype)


def combine(blocks, places, shares):
    return pl.pallas_call(
        functools.partial(combine_kernel, len(blocks)),
        out_shape=jax.ShapeDtypeStruct((shares.shape[0], blocks[0].shape[1]), jnp.bfloat16),
    )(*blocks, places, shares)


def body(
    moe_rows,
    routes,
    gate_weights,
    gate_weight,
    up_weight,
    down_weight,
    queries,
    latent_cache,
    lengths,
):
    devices = lax.axis_size("ep")
    experts = devices // SPLIT
    outer_size = experts // 2
    row_count, model_width = moe_rows.shape
    top_count = routes.shape[1]
    capacity = 2 * row_count * top_count * SPLIT // devices
    me = lax.axis_index("ep")
    outer, inner = me // 8, me // 4 % 2

    def send(array, far=0, near=0, swap_x=0, swap_core=0):
        return lax.ppermute(array, "ep", permutation(devices, far, near, swap_x, swap_core))

    flat_routes = routes.reshape(-1)
    relative = (flat_routes // 2 - outer + outer_size) % outer_size * 2 + ((flat_routes % 2) ^ inner)
    onehot = (relative[:, None] == jnp.arange(experts, dtype=jnp.int32)[None, :]).astype(jnp.int32)
    earlier = jnp.cumsum(onehot, axis=0) - onehot
    slot_ids = jnp.sum(earlier * onehot, axis=1)
    targets = (relative * capacity + slot_ids).reshape(row_count, top_count)
    placing = targets[:, :, None] == jnp.arange(experts * capacity, dtype=jnp.int32)[None, None, :]
    spread = jnp.any(placing, axis=1).astype(jnp.bfloat16)
    outgoing = jnp.einsum(
        "rp,rd->pd", spread, moe_rows, preferred_element_type=jnp.float32
    ).astype(jnp.bfloat16)
    places = placing.astype(jnp.bfloat16).transpose(1, 0, 2)

    def outgoing_block(far, near):
        at = (far * 2 + near) * capacity
        return outgoing[at : at + capacity]

    close = sorted({1, outer_size - 1} - {0})
    rest = [(f, n) for f in range(2, outer_size - 1) for n in range(2)]
    own, near = [(0, 0)], [(0, 1)] + [(close[0], n) for n in range(2)]
    last = [(close[1], n) for n in range(2)]
    rows, crossed = {(0, 0): outgoing_block(0, 0)}, {}

    def step(key, *first):
        rows[key] = send(after(outgoing_block(*key), *first), *key)

    def cross(keys, *first):
        together = jnp.concatenate([rows[key] for key in keys], axis=0)
        crossed[keys[0]] = send(after(together, *first) if first else together, swap_x=1)

    gate_other = send(gate_weight, swap_core=1)
    up_other = send(up_weight, swap_core=1)
    for key in rest:
        step(key)
    cross(own)
    begun = [gate_other, up_other, crossed[0, 0]] + [rows[key] for key in rest]
    cross(rest, *begun)
    for key in near:
        step(key, *begun)
    down_other = send(after(down_weight, *begun), swap_core=1)
    begun = [crossed[rest[0]], down_other] + [rows[key] for key in near]
    for key in last:
        step(key, *begun)
    cross(near, *begun)

    mine, theirs = {}, {}

    def run(*groups):
        keys = [key for group in groups for key in group]
        blocks = [rows[key] for key in keys] + [crossed[group[0]] for group in groups]
        outs = expert(
            blocks, (gate_weight, gate_other), (up_weight, up_other), (down_weight, down_other)
        )
        mine.update(zip(keys, outs))
        theirs.update(zip([group[0] for group in groups], outs[len(keys) :]))

    back, returned = {}, {}

    def finish(keys, *first):
        came = after(back[keys[0]], *first)
        for i, key in enumerate(keys):
            part = came[i * capacity : (i + 1) * capacity]
            total = (mine[key].astype(jnp.float32) + part.astype(jnp.float32)).astype(jnp.bfloat16)
            returned[key] = total if key == (0, 0) else send(total, -key[0], key[1])

    run(own, rest)
    back[rest[0]] = send(theirs[rest[0]], swap_x=1)
    cross(last, theirs[rest[0]], crossed[near[0]])
    run(near)
    back[near[0]] = send(theirs[near[0]], swap_x=1)
    finish(rest)
    run(last)
    back[last[0]] = send(after(theirs[last[0]], *(returned[key] for key in rest)), swap_x=1)
    back[own[0]] = send(after(theirs[own[0]], back[near[0]]), swap_x=1)
    for group in (near, last):
        finish(group)
    finish(own, returned[near[1]])
    moe_out = combine(
        [returned[f, n] for f in range(outer_size) for n in range(2)], places, gate_weights
    )
    attn_out = attention(queries, latent_cache, lengths)
    return (moe_out, attn_out)


def solution(mesh):
    in_specs = (
        P(("groups", "ep"), None),
        P(("groups", "ep"), None),
        P(("groups", "ep"), None),
        P(None, "ep"),
        P(None, "ep"),
        P("ep", None),
        P(("groups", "ep"), None, None),
        P(("groups", "ep"), None, None),
        P(("groups", "ep")),
    )
    out_specs = (P(("groups", "ep"), None), P(("groups", "ep"), None, None))
    return jax.shard_map(body, mesh=mesh, in_specs=in_specs, out_specs=out_specs, check_vma=False)
```

```python
import functools

import jax
import jax.numpy as jnp
from jax import lax
from jax.experimental import pallas as pl
from jax.experimental.pallas import tpu as pltpu
from jax.sharding import PartitionSpec as P

SPLIT = 4
NOPE = 512

softmax_scale = 192.0 ** (-0.5)


def attention(queries, latent_cache, lengths):
    scores = (
        jnp.einsum("rhc,rlc->rhl", queries, latent_cache, preferred_element_type=jnp.float32)
        * softmax_scale
    )
    positions = jnp.arange(latent_cache.shape[1], dtype=jnp.int32)
    valid_mask = positions[None, None, :] < lengths[:, None, None]
    scores = jnp.where(valid_mask, scores, -1e30)
    highest = jnp.max(scores, axis=-1, keepdims=True)
    expons = jnp.where(valid_mask, jnp.exp(scores - highest), 0.0)
    weights = (expons / jnp.sum(expons, axis=-1, keepdims=True)).astype(jnp.bfloat16)
    return jnp.einsum(
        "rhl,rlc->rhc", weights, latent_cache[:, :, :NOPE], preferred_element_type=jnp.float32
    ).astype(jnp.bfloat16)


def permutation(devices, far, near, swap_x, swap_core):
    outer_size = devices // 8
    pairs = []
    for source in range(devices):
        outer, inner, x, core = source // 8, source // 4 % 2, source // 2 % 2, source % 2
        target = ((outer + far) % outer_size * 2 + (inner ^ near)) * 4 + (x ^ swap_x) * 2 + (core ^ swap_core)
        pairs.append((source, target))
    return pairs


def after(array, *first):
    return lax.optimization_barrier((array,) + first)[0]


def expert_kernel(number, counts, parts, *refs):
    blocks, weights, outs = refs[:number], refs[number : number + 6], refs[number + 6 : -5]
    wide, tall, total, hidden, arrived = refs[-5:]
    model_width, width = weights[0].shape
    part_width = model_width // parts
    spans = [slice(p * part_width, (p + 1) * part_width) for p in range(parts)]
    wide_copies = [
        [
            pltpu.make_async_copy(weights[i].at[span], wide.at[i, span], arrived.at[p * 6 + i])
            for i in range(4)
        ]
        for p, span in enumerate(spans)
    ]
    tall_copies = [
        [
            pltpu.make_async_copy(
                weights[4 + i].at[:, span], tall.at[i, :, span], arrived.at[p * 6 + 4 + i]
            )
            for i in range(2)
        ]
        for p, span in enumerate(spans)
    ]
    for copies in wide_copies + tall_copies:
        for copy in copies:
            copy.start()
    for p, span in enumerate(spans):
        rows = jnp.concatenate([b[:, span] for b in blocks], axis=0)
        for i in range(4):
            wide_copies[p][i].wait()
            product = jnp.dot(rows, wide[i, span], preferred_element_type=jnp.float32)
            columns = slice(i * width, (i + 1) * width)
            total[:, columns] = product if p == 0 else total[:, columns] + product
    gate, up = total[:, : 2 * width], total[:, 2 * width :]
    hidden[...] = (gate / (1.0 + jnp.exp(-gate)) * up).astype(jnp.bfloat16)
    piece = part_width // 4
    for p in range(parts):
        for copy in tall_copies[p]:
            copy.wait()
        for q in range(4):
            columns = slice(p * part_width + q * piece, p * part_width + (q + 1) * piece)
            part = jnp.dot(
                hidden[:, :width], tall[0, :, columns], preferred_element_type=jnp.float32
            )
            part += jnp.dot(
                hidden[:, width:], tall[1, :, columns], preferred_element_type=jnp.float32
            )
            part = part.astype(jnp.bfloat16)
            at = 0
            for count, out in zip(counts, outs):
                out[:, columns] = part[at : at + count]
                at += count


def expert(blocks, counts, gates, ups, downs):
    model_width, width = gates[0].shape
    slots, parts = sum(counts), 2
    return pl.pallas_call(
        functools.partial(expert_kernel, len(blocks), counts, parts),
        in_specs=[pl.BlockSpec(memory_space=pltpu.VMEM)] * len(blocks)
        + [pl.BlockSpec(memory_space=pl.ANY)] * 6,
        out_specs=[pl.BlockSpec(memory_space=pltpu.VMEM)] * len(counts),
        out_shape=[jax.ShapeDtypeStruct((c, model_width), jnp.bfloat16) for c in counts],
        scratch_shapes=[
            pltpu.VMEM((4, model_width, width), jnp.bfloat16),
            pltpu.VMEM((2, width, model_width), jnp.bfloat16),
            pltpu.VMEM((slots, 4 * width), jnp.float32),
            pltpu.VMEM((slots, 2 * width), jnp.bfloat16),
            pltpu.SemaphoreType.DMA((6 * parts,)),
        ],
        compiler_params=pltpu.CompilerParams(vmem_limit_bytes=60 * 1024 * 1024),
        cost_estimate=pl.CostEstimate(
            flops=12 * slots * model_width * width,
            bytes_accessed=12 * model_width * width + 4 * slots * model_width,
            transcendentals=2 * slots * width,
        ),
    )(*blocks, *gates, *ups, *downs)


def combine_kernel(number, *refs):
    blocks, (places, shares, out) = refs[:number], refs[number:]
    model_width = out.shape[1]
    piece = model_width // 7
    for lo in range(0, model_width, piece):
        columns = slice(lo, lo + piece)
        rows = jnp.concatenate([b[:, columns] for b in blocks], axis=0)
        total = 0.0
        for k in range(shares.shape[1]):
            picked = jnp.dot(places[k], rows, preferred_element_type=jnp.float32)
            total = total + picked * shares[:, k : k + 1]
        out[:, columns] = total.astype(out.dtype)


def combine(blocks, places, shares):
    return pl.pallas_call(
        functools.partial(combine_kernel, len(blocks)),
        out_shape=jax.ShapeDtypeStruct((shares.shape[0], blocks[0].shape[1]), jnp.bfloat16),
    )(*blocks, places, shares)


def body(
    moe_rows,
    routes,
    gate_weights,
    gate_weight,
    up_weight,
    down_weight,
    queries,
    latent_cache,
    lengths,
):
    devices = lax.axis_size("ep")
    experts = devices // SPLIT
    outer_size = experts // 2
    row_count, model_width = moe_rows.shape
    top_count = routes.shape[1]
    capacity = 2 * row_count * top_count * SPLIT // devices
    me = lax.axis_index("ep")
    outer, inner = me // 8, me // 4 % 2

    def send(array, far=0, near=0, swap_x=0, swap_core=0):
        return lax.ppermute(array, "ep", permutation(devices, far, near, swap_x, swap_core))

    flat_routes = routes.reshape(-1)
    relative = (flat_routes // 2 - outer + outer_size) % outer_size * 2 + ((flat_routes % 2) ^ inner)
    onehot = (relative[:, None] == jnp.arange(experts, dtype=jnp.int32)[None, :]).astype(jnp.int32)
    earlier = jnp.cumsum(onehot, axis=0) - onehot
    slot_ids = jnp.sum(earlier * onehot, axis=1)
    targets = (relative * capacity + slot_ids).reshape(row_count, top_count)
    placing = targets[:, :, None] == jnp.arange(experts * capacity, dtype=jnp.int32)[None, None, :]
    spread = jnp.any(placing, axis=1).astype(jnp.bfloat16)
    outgoing = jnp.einsum(
        "rp,rd->pd", spread, moe_rows, preferred_element_type=jnp.float32
    ).astype(jnp.bfloat16)
    places = placing.astype(jnp.bfloat16).transpose(1, 0, 2)

    def outgoing_block(far, near):
        at = (far * 2 + near) * capacity
        return outgoing[at : at + capacity]

    close = sorted({1, outer_size - 1} - {0})
    rest = [(f, n) for f in range(2, outer_size - 1) for n in range(2)]
    own, near = [(0, 0)], [(0, 1)] + [(close[0], n) for n in range(2)]
    last = [(close[1], n) for n in range(2)]
    rows, crossed = {(0, 0): outgoing_block(0, 0)}, {}

    def step(key, *first):
        rows[key] = send(after(outgoing_block(*key), *first), *key)

    def cross(keys, *first):
        together = jnp.concatenate([rows[key] for key in keys], axis=0)
        crossed[keys[0]] = send(after(together, *first) if first else together, swap_x=1)

    gate_other = send(gate_weight, swap_core=1)
    up_other = send(up_weight, swap_core=1)
    for key in rest:
        step(key)
    cross(own)
    begun = [gate_other, up_other, crossed[0, 0]] + [rows[key] for key in rest]
    cross(rest, *begun)
    for key in near:
        step(key, *begun)
    down_other = send(after(down_weight, *begun), swap_core=1)
    begun = [crossed[rest[0]], down_other] + [rows[key] for key in near]
    for key in last:
        step(key, *begun)
    cross(near, *begun)

    mine, theirs = {}, {}

    def run(*groups, returns=None):
        keys = [key for group in groups for key in group]
        returns = returns or groups
        blocks = [rows[key] for key in keys] + [crossed[group[0]] for group in groups]
        outs = expert(
            blocks,
            (capacity,) * len(keys) + tuple(capacity * len(group) for group in returns),
            (gate_weight, gate_other),
            (up_weight, up_other),
            (down_weight, down_other),
        )
        mine.update(zip(keys, outs))
        theirs.update(zip([group[0] for group in returns], outs[len(keys) :]))

    back, returned = {}, {}

    def give_back(keys, *first):
        back[keys[0]] = send(after(theirs[keys[0]], *first), swap_x=1)

    def finish(keys, *first):
        came = after(back[keys[0]], *first)
        for i, key in enumerate(keys):
            part = came[i * capacity : (i + 1) * capacity]
            total = (mine[key].astype(jnp.float32) + part.astype(jnp.float32)).astype(jnp.bfloat16)
            returned[key] = total if key == (0, 0) else send(total, -key[0], key[1])

    run(own, rest)
    give_back(rest)
    cross(last, theirs[rest[0]], crossed[near[0]])
    run(near)
    give_back(near)
    finish(rest, mine[near[0]])
    singles = [[key] for key in last]
    run(last, returns=singles)
    for keys in singles:
        give_back(keys, back[near[0]], *(returned[key] for key in rest))
    give_back(own, back[near[0]])
    for keys in [near] + singles:
        finish(keys)
    finish(own, returned[near[1]])
    moe_out = combine(
        [returned[f, n] for f in range(outer_size) for n in range(2)], places, gate_weights
    )
    attn_out = attention(queries, latent_cache, lengths)
    return (moe_out, attn_out)


def solution(mesh):
    in_specs = (
        P(("groups", "ep"), None),
        P(("groups", "ep"), None),
        P(("groups", "ep"), None),
        P(None, "ep"),
        P(None, "ep"),
        P("ep", None),
        P(("groups", "ep"), None, None),
        P(("groups", "ep"), None, None),
        P(("groups", "ep")),
    )
    out_specs = (P(("groups", "ep"), None), P(("groups", "ep"), None, None))
    return jax.shard_map(body, mesh=mesh, in_specs=in_specs, out_specs=out_specs, check_vma=False)
```

```python
import functools

import jax
import jax.numpy as jnp
from jax import lax
from jax.experimental import pallas as pl
from jax.experimental.pallas import tpu as pltpu
from jax.sharding import PartitionSpec as P

SPLIT = 4
NOPE = 512

softmax_scale = 192.0 ** (-0.5)


def attention(queries, latent_cache, lengths):
    scores = (
        jnp.einsum("rhc,rlc->rhl", queries, latent_cache, preferred_element_type=jnp.float32)
        * softmax_scale
    )
    positions = jnp.arange(latent_cache.shape[1], dtype=jnp.int32)
    valid_mask = positions[None, None, :] < lengths[:, None, None]
    scores = jnp.where(valid_mask, scores, -1e30)
    highest = jnp.max(scores, axis=-1, keepdims=True)
    expons = jnp.where(valid_mask, jnp.exp(scores - highest), 0.0)
    weights = (expons / jnp.sum(expons, axis=-1, keepdims=True)).astype(jnp.bfloat16)
    return jnp.einsum(
        "rhl,rlc->rhc", weights, latent_cache[:, :, :NOPE], preferred_element_type=jnp.float32
    ).astype(jnp.bfloat16)


def permutation(devices, far, near, swap_x, swap_core):
    outer_size = devices // 8
    pairs = []
    for source in range(devices):
        outer, inner, x, core = source // 8, source // 4 % 2, source // 2 % 2, source % 2
        target = ((outer + far) % outer_size * 2 + (inner ^ near)) * 4 + (x ^ swap_x) * 2 + (core ^ swap_core)
        pairs.append((source, target))
    return pairs


def after(array, *first):
    return lax.optimization_barrier((array,) + first)[0]


def expert_kernel(number, counts, parts, *refs):
    blocks, weights, outs = refs[:number], refs[number : number + 6], refs[number + 6 : -5]
    wide, tall, total, hidden, arrived = refs[-5:]
    model_width, width = weights[0].shape
    part_width = model_width // parts
    spans = [slice(p * part_width, (p + 1) * part_width) for p in range(parts)]
    wide_copies = [
        [
            pltpu.make_async_copy(weights[i].at[span], wide.at[i, span], arrived.at[p * 6 + i])
            for i in range(4)
        ]
        for p, span in enumerate(spans)
    ]
    tall_copies = [
        [
            pltpu.make_async_copy(
                weights[4 + i].at[:, span], tall.at[i, :, span], arrived.at[p * 6 + 4 + i]
            )
            for i in range(2)
        ]
        for p, span in enumerate(spans)
    ]
    for copies in wide_copies + tall_copies:
        for copy in copies:
            copy.start()
    for p, span in enumerate(spans):
        rows = jnp.concatenate([b[:, span] for b in blocks], axis=0)
        for i in range(4):
            wide_copies[p][i].wait()
            product = jnp.dot(rows, wide[i, span], preferred_element_type=jnp.float32)
            columns = slice(i * width, (i + 1) * width)
            total[:, columns] = product if p == 0 else total[:, columns] + product
    gate, up = total[:, : 2 * width], total[:, 2 * width :]
    hidden[...] = (gate / (1.0 + jnp.exp(-gate)) * up).astype(jnp.bfloat16)
    piece = part_width // 4
    for p in range(parts):
        for copy in tall_copies[p]:
            copy.wait()
        for q in range(4):
            columns = slice(p * part_width + q * piece, p * part_width + (q + 1) * piece)
            part = jnp.dot(
                hidden[:, :width], tall[0, :, columns], preferred_element_type=jnp.float32
            )
            part += jnp.dot(
                hidden[:, width:], tall[1, :, columns], preferred_element_type=jnp.float32
            )
            part = part.astype(jnp.bfloat16)
            at = 0
            for count, out in zip(counts, outs):
                out[:, columns] = part[at : at + count]
                at += count


def expert(blocks, counts, gates, ups, downs):
    model_width, width = gates[0].shape
    slots, parts = sum(counts), 2
    return pl.pallas_call(
        functools.partial(expert_kernel, len(blocks), counts, parts),
        in_specs=[pl.BlockSpec(memory_space=pltpu.VMEM)] * len(blocks)
        + [pl.BlockSpec(memory_space=pl.ANY)] * 6,
        out_specs=[pl.BlockSpec(memory_space=pltpu.VMEM)] * len(counts),
        out_shape=[jax.ShapeDtypeStruct((c, model_width), jnp.bfloat16) for c in counts],
        scratch_shapes=[
            pltpu.VMEM((4, model_width, width), jnp.bfloat16),
            pltpu.VMEM((2, width, model_width), jnp.bfloat16),
            pltpu.VMEM((slots, 4 * width), jnp.float32),
            pltpu.VMEM((slots, 2 * width), jnp.bfloat16),
            pltpu.SemaphoreType.DMA((6 * parts,)),
        ],
        compiler_params=pltpu.CompilerParams(vmem_limit_bytes=60 * 1024 * 1024),
        cost_estimate=pl.CostEstimate(
            flops=12 * slots * model_width * width,
            bytes_accessed=12 * model_width * width + 4 * slots * model_width,
            transcendentals=2 * slots * width,
        ),
    )(*blocks, *gates, *ups, *downs)


def combine_kernel(number, start, *refs):
    blocks, (places, shares), out = refs[:number], refs[number : number + 2], refs[-1]
    model_width = out.shape[1]
    piece = model_width // 7
    for lo in range(0, model_width, piece):
        columns = slice(lo, lo + piece)
        rows = jnp.concatenate([b[:, columns] for b in blocks], axis=0)
        total = refs[number + 2][:, columns] if start else 0.0
        for k in range(shares.shape[1]):
            picked = jnp.dot(places[k], rows, preferred_element_type=jnp.float32)
            total = total + picked * shares[:, k : k + 1]
        out[:, columns] = total.astype(out.dtype)


def combine(blocks, places, shares, dtype, *start):
    return pl.pallas_call(
        functools.partial(combine_kernel, len(blocks), bool(start)),
        out_shape=jax.ShapeDtypeStruct((shares.shape[0], blocks[0].shape[1]), dtype),
    )(*blocks, places, shares, *start)


def body(
    moe_rows,
    routes,
    gate_weights,
    gate_weight,
    up_weight,
    down_weight,
    queries,
    latent_cache,
    lengths,
):
    devices = lax.axis_size("ep")
    experts = devices // SPLIT
    outer_size = experts // 2
    row_count, model_width = moe_rows.shape
    top_count = routes.shape[1]
    capacity = 2 * row_count * top_count * SPLIT // devices
    me = lax.axis_index("ep")
    outer, inner = me // 8, me // 4 % 2

    def send(array, far=0, near=0, swap_x=0, swap_core=0):
        return lax.ppermute(array, "ep", permutation(devices, far, near, swap_x, swap_core))

    flat_routes = routes.reshape(-1)
    relative = (flat_routes // 2 - outer + outer_size) % outer_size * 2 + ((flat_routes % 2) ^ inner)
    onehot = (relative[:, None] == jnp.arange(experts, dtype=jnp.int32)[None, :]).astype(jnp.int32)
    earlier = jnp.cumsum(onehot, axis=0) - onehot
    slot_ids = jnp.sum(earlier * onehot, axis=1)
    targets = (relative * capacity + slot_ids).reshape(row_count, top_count)
    slots = jnp.arange(experts * capacity, dtype=jnp.int32)[None, None, :]
    spread = jnp.any(targets[:, :, None] == slots, axis=1).astype(jnp.bfloat16)
    outgoing = jnp.einsum(
        "rp,rd->pd", spread, moe_rows, preferred_element_type=jnp.float32
    ).astype(jnp.bfloat16)

    def outgoing_block(far, near):
        at = (far * 2 + near) * capacity
        return outgoing[at : at + capacity]

    close = sorted({1, outer_size - 1} - {0})
    rest = [(f, n) for f in range(2, outer_size - 1) for n in range(2)]
    own, near = [(0, 0), (0, 1)], [(close[0], n) for n in range(2)]
    last = [(close[1], n) for n in range(2)]
    rows, crossed = {(0, 0): outgoing_block(0, 0)}, {}

    def step(key, *first):
        rows[key] = send(after(outgoing_block(*key), *first), *key)

    def cross(keys, *first):
        together = jnp.concatenate([rows[key] for key in keys], axis=0)
        crossed[keys[0]] = send(after(together, *first) if first else together, swap_x=1)

    gate_other = send(gate_weight, swap_core=1)
    up_other = send(up_weight, swap_core=1)
    for key in [(0, 1)] + rest:
        step(key)
    begun = [gate_other, up_other, rows[0, 1]] + [rows[key] for key in rest]
    cross(rest, *begun)
    cross(own, *begun)
    for key in near:
        step(key, *begun)
    down_other = send(after(down_weight, *begun), swap_core=1)
    begun = [crossed[rest[0]], down_other] + [rows[key] for key in near]
    for key in last:
        step(key, *begun)
    cross(near, *begun)

    mine, theirs = {}, {}

    def run(groups, returns):
        keys = [key for group in groups for key in group]
        blocks = [rows[key] for key in keys] + [crossed[group[0]] for group in groups]
        outs = expert(
            blocks,
            (capacity,) * len(keys) + tuple(capacity * len(group) for group in returns),
            (gate_weight, gate_other),
            (up_weight, up_other),
            (down_weight, down_other),
        )
        mine.update(zip(keys, outs))
        theirs.update(zip([group[0] for group in returns], outs[len(keys) :]))

    back, returned = {}, {}

    def give_back(keys, *first):
        back[keys[0]] = send(after(theirs[keys[0]], *first), swap_x=1)

    def finish(keys, *first):
        came = after(back[keys[0]], *first)
        for i, key in enumerate(keys):
            part = came[i * capacity : (i + 1) * capacity]
            total = (mine[key].astype(jnp.float32) + part.astype(jnp.float32)).astype(jnp.bfloat16)
            returned[key] = total if key == (0, 0) else send(total, -key[0], key[1])

    run([rest], [rest])
    give_back(rest)
    cross(last, theirs[rest[0]], crossed[own[0]])
    run([own, near], [own, near])
    give_back(near)
    give_back(own)
    finish(rest, mine[near[0]])
    singles = [[key] for key in last]
    run([last], singles)
    for keys in singles:
        give_back(keys, back[near[0]], *(returned[key] for key in rest))
    for keys in [near] + singles:
        finish(keys)
    finish(own, returned[near[0]])

    places = after(targets, theirs[near[0]])[:, :, None] == slots
    places = places.astype(jnp.bfloat16).transpose(1, 0, 2)

    def gather(keys, dtype, *start):
        columns = [
            places[:, :, (f * 2 + n) * capacity : (f * 2 + n + 1) * capacity] for f, n in keys
        ]
        return combine(
            [returned[key] for key in keys],
            jnp.concatenate(columns, axis=2),
            gate_weights,
            dtype,
            *start,
        )

    most = gather(own + rest + near, jnp.float32)
    moe_out = gather(last, jnp.bfloat16, most)
    attn_out = attention(after(queries, theirs[last[0]]), latent_cache, lengths)
    return (moe_out, attn_out)


def solution(mesh):
    in_specs = (
        P(("groups", "ep"), None),
        P(("groups", "ep"), None),
        P(("groups", "ep"), None),
        P(None, "ep"),
        P(None, "ep"),
        P("ep", None),
        P(("groups", "ep"), None, None),
        P(("groups", "ep"), None, None),
        P(("groups", "ep")),
    )
    out_specs = (P(("groups", "ep"), None), P(("groups", "ep"), None, None))
    return jax.shard_map(body, mesh=mesh, in_specs=in_specs, out_specs=out_specs, check_vma=False)
```

```python
import functools

import jax
import jax.numpy as jnp
from jax import lax
from jax.experimental import pallas as pl
from jax.experimental.pallas import tpu as pltpu
from jax.sharding import PartitionSpec as P

SPLIT = 4
NOPE = 512

softmax_scale = 192.0 ** (-0.5)


def attention(queries, latent_cache, lengths):
    scores = (
        jnp.einsum("rhc,rlc->rhl", queries, latent_cache, preferred_element_type=jnp.float32)
        * softmax_scale
    )
    positions = jnp.arange(latent_cache.shape[1], dtype=jnp.int32)
    valid_mask = positions[None, None, :] < lengths[:, None, None]
    scores = jnp.where(valid_mask, scores, -1e30)
    highest = jnp.max(scores, axis=-1, keepdims=True)
    expons = jnp.where(valid_mask, jnp.exp(scores - highest), 0.0)
    weights = (expons / jnp.sum(expons, axis=-1, keepdims=True)).astype(jnp.bfloat16)
    return jnp.einsum(
        "rhl,rlc->rhc", weights, latent_cache[:, :, :NOPE], preferred_element_type=jnp.float32
    ).astype(jnp.bfloat16)


def permutation(devices, far, near, swap_x, swap_core):
    outer_size = devices // 8
    pairs = []
    for source in range(devices):
        outer, inner, x, core = source // 8, source // 4 % 2, source // 2 % 2, source % 2
        target = ((outer + far) % outer_size * 2 + (inner ^ near)) * 4 + (x ^ swap_x) * 2 + (core ^ swap_core)
        pairs.append((source, target))
    return pairs


def after(array, *first):
    return lax.optimization_barrier((array,) + first)[0]


def expert_kernel(number, counts, parts, *refs):
    blocks, weights, outs = refs[:number], refs[number : number + 6], refs[number + 6 : -5]
    wide, tall, total, hidden, arrived = refs[-5:]
    model_width, width = weights[0].shape
    part_width = model_width // parts
    spans = [slice(p * part_width, (p + 1) * part_width) for p in range(parts)]
    wide_copies = [
        [
            pltpu.make_async_copy(weights[i].at[span], wide.at[i, span], arrived.at[p * 6 + i])
            for i in range(4)
        ]
        for p, span in enumerate(spans)
    ]
    tall_copies = [
        [
            pltpu.make_async_copy(
                weights[4 + i].at[:, span], tall.at[i, :, span], arrived.at[p * 6 + 4 + i]
            )
            for i in range(2)
        ]
        for p, span in enumerate(spans)
    ]
    for copies in wide_copies + tall_copies:
        for copy in copies:
            copy.start()
    for p, span in enumerate(spans):
        rows = jnp.concatenate([b[:, span] for b in blocks], axis=0)
        for i in range(4):
            wide_copies[p][i].wait()
            product = jnp.dot(rows, wide[i, span], preferred_element_type=jnp.float32)
            columns = slice(i * width, (i + 1) * width)
            total[:, columns] = product if p == 0 else total[:, columns] + product
    gate, up = total[:, : 2 * width], total[:, 2 * width :]
    hidden[...] = (gate / (1.0 + jnp.exp(-gate)) * up).astype(jnp.bfloat16)
    piece = part_width // 4
    for p in range(parts):
        for copy in tall_copies[p]:
            copy.wait()
        for q in range(4):
            columns = slice(p * part_width + q * piece, p * part_width + (q + 1) * piece)
            part = jnp.dot(
                hidden[:, :width], tall[0, :, columns], preferred_element_type=jnp.float32
            )
            part += jnp.dot(
                hidden[:, width:], tall[1, :, columns], preferred_element_type=jnp.float32
            )
            part = part.astype(jnp.bfloat16)
            at = 0
            for count, out in zip(counts, outs):
                out[:, columns] = part[at : at + count]
                at += count


def expert(blocks, counts, gates, ups, downs):
    model_width, width = gates[0].shape
    slots, parts = sum(counts), 2
    return pl.pallas_call(
        functools.partial(expert_kernel, len(blocks), counts, parts),
        in_specs=[pl.BlockSpec(memory_space=pltpu.VMEM)] * len(blocks)
        + [pl.BlockSpec(memory_space=pl.ANY)] * 6,
        out_specs=[pl.BlockSpec(memory_space=pltpu.VMEM)] * len(counts),
        out_shape=[jax.ShapeDtypeStruct((c, model_width), jnp.bfloat16) for c in counts],
        scratch_shapes=[
            pltpu.VMEM((4, model_width, width), jnp.bfloat16),
            pltpu.VMEM((2, width, model_width), jnp.bfloat16),
            pltpu.VMEM((slots, 4 * width), jnp.float32),
            pltpu.VMEM((slots, 2 * width), jnp.bfloat16),
            pltpu.SemaphoreType.DMA((6 * parts,)),
        ],
        compiler_params=pltpu.CompilerParams(vmem_limit_bytes=60 * 1024 * 1024),
        cost_estimate=pl.CostEstimate(
            flops=12 * slots * model_width * width,
            bytes_accessed=12 * model_width * width + 4 * slots * model_width,
            transcendentals=2 * slots * width,
        ),
    )(*blocks, *gates, *ups, *downs)


def combine_kernel(number, start, *refs):
    blocks, (places, shares), out = refs[:number], refs[number : number + 2], refs[-1]
    model_width = out.shape[1]
    piece = model_width // 7
    for lo in range(0, model_width, piece):
        columns = slice(lo, lo + piece)
        rows = jnp.concatenate([b[:, columns] for b in blocks], axis=0)
        total = refs[number + 2][:, columns] if start else 0.0
        for k in range(shares.shape[1]):
            picked = jnp.dot(places[k], rows, preferred_element_type=jnp.float32)
            total = total + picked * shares[:, k : k + 1]
        out[:, columns] = total.astype(out.dtype)


def combine(blocks, places, shares, dtype, *start):
    return pl.pallas_call(
        functools.partial(combine_kernel, len(blocks), bool(start)),
        out_shape=jax.ShapeDtypeStruct((shares.shape[0], blocks[0].shape[1]), dtype),
    )(*blocks, places, shares, *start)


def body(
    moe_rows,
    routes,
    gate_weights,
    gate_weight,
    up_weight,
    down_weight,
    queries,
    latent_cache,
    lengths,
):
    devices = lax.axis_size("ep")
    experts = devices // SPLIT
    outer_size = experts // 2
    row_count, model_width = moe_rows.shape
    top_count = routes.shape[1]
    capacity = 2 * row_count * top_count * SPLIT // devices
    me = lax.axis_index("ep")
    outer, inner = me // 8, me // 4 % 2

    def send(array, far=0, near=0, swap_x=0, swap_core=0):
        return lax.ppermute(array, "ep", permutation(devices, far, near, swap_x, swap_core))

    flat_routes = routes.reshape(-1)
    relative = (flat_routes // 2 - outer + outer_size) % outer_size * 2 + ((flat_routes % 2) ^ inner)
    onehot = (relative[:, None] == jnp.arange(experts, dtype=jnp.int32)[None, :]).astype(jnp.int32)
    earlier = jnp.cumsum(onehot, axis=0) - onehot
    slot_ids = jnp.sum(earlier * onehot, axis=1)
    targets = (relative * capacity + slot_ids).reshape(row_count, top_count)
    slots = jnp.arange(experts * capacity, dtype=jnp.int32)[None, None, :]
    spread = jnp.any(targets[:, :, None] == slots, axis=1).astype(jnp.bfloat16)
    outgoing = jnp.einsum(
        "rp,rd->pd", spread, moe_rows, preferred_element_type=jnp.float32
    ).astype(jnp.bfloat16)

    def outgoing_block(far, near):
        at = (far * 2 + near) * capacity
        return outgoing[at : at + capacity]

    close = sorted({1, outer_size - 1} - {0})
    rest = [(f, n) for f in range(2, outer_size - 1) for n in range(2)]
    near = [(close[0], n) for n in range(2)]
    last = [(close[1], n) for n in range(2)]
    rows, crossed = {(0, 0): outgoing_block(0, 0)}, {}

    def step(key, *first):
        rows[key] = send(after(outgoing_block(*key), *first), *key)

    def cross(keys, *first):
        together = jnp.concatenate([rows[key] for key in keys], axis=0)
        crossed[keys[0]] = send(after(together, *first) if first else together, swap_x=1)

    gate_other = send(gate_weight, swap_core=1)
    up_other = send(up_weight, swap_core=1)
    for key in rest:
        step(key)
    beside = send(outgoing[: 2 * capacity], swap_x=1)
    begun = [gate_other, up_other, beside] + [rows[key] for key in rest]
    cross(rest, *begun)
    pair = jnp.concatenate([outgoing_block(0, 1), beside[capacity:]], axis=0)
    pair = send(after(pair, *begun), near=1)
    for key in near:
        step(key, *begun)
    down_other = send(after(down_weight, *begun), swap_core=1)
    begun = [crossed[rest[0]], down_other, pair] + [rows[key] for key in near]
    for key in last:
        step(key, *begun)
    cross(near, *begun)

    mine, theirs = {}, {}

    def run(groups, returns, *others):
        keys = [key for group in groups for key in group]
        blocks = [rows[key] for key in keys] + [crossed[group[0]] for group in groups]
        counts = (capacity,) * len(keys) + tuple(capacity * len(group) for group in returns)
        outs = expert(
            blocks + list(others),
            counts + tuple(other.shape[0] for other in others),
            (gate_weight, gate_other),
            (up_weight, up_other),
            (down_weight, down_other),
        )
        mine.update(zip(keys, outs))
        theirs.update(zip([group[0] for group in returns], outs[len(keys) :]))
        return outs[len(counts) :]

    back, returned = {}, {}

    def give_back(keys, *first):
        back[keys[0]] = send(after(theirs[keys[0]], *first), swap_x=1)

    def add(one, other):
        return (one.astype(jnp.float32) + other.astype(jnp.float32)).astype(jnp.bfloat16)

    def finish(keys, *first):
        came = after(back[keys[0]], *first)
        for i, key in enumerate(keys):
            total = add(mine[key], came[i * capacity : (i + 1) * capacity])
            returned[key] = send(total, -key[0], key[1])

    run([rest], [rest])
    give_back(rest)
    cross(last, theirs[rest[0]])
    own_mine, own_theirs, own_pair = run(
        [near], [near], rows[0, 0], beside[:capacity], pair
    )
    give_back(near)
    own_pair = send(own_pair, near=1)
    finish(rest, mine[near[0]])
    singles = [[key] for key in last]
    run([last], singles)
    for keys in singles:
        give_back(keys, back[near[0]], *(returned[key] for key in rest))
    own_back = send(jnp.concatenate([own_theirs, own_pair[capacity:]], axis=0), swap_x=1)
    for keys in [near] + singles:
        finish(keys)
    own_back = after(own_back, returned[near[0]])
    returned[0, 0] = add(own_mine, own_back[:capacity])
    returned[0, 1] = add(own_pair[:capacity], own_back[capacity:])

    places = after(targets, theirs[near[0]])[:, :, None] == slots
    places = places.astype(jnp.bfloat16).transpose(1, 0, 2)

    def gather(keys, dtype, *start):
        columns = [
            places[:, :, (f * 2 + n) * capacity : (f * 2 + n + 1) * capacity] for f, n in keys
        ]
        return combine(
            [returned[key] for key in keys],
            jnp.concatenate(columns, axis=2),
            gate_weights,
            dtype,
            *start,
        )

    most = gather(rest + near, jnp.float32)
    moe_out = gather([(0, 0), (0, 1)] + last, jnp.bfloat16, most)
    attn_out = attention(after(queries, back[last[0]]), latent_cache, lengths)
    return (moe_out, attn_out)


def solution(mesh):
    in_specs = (
        P(("groups", "ep"), None),
        P(("groups", "ep"), None),
        P(("groups", "ep"), None),
        P(None, "ep"),
        P(None, "ep"),
        P("ep", None),
        P(("groups", "ep"), None, None),
        P(("groups", "ep"), None, None),
        P(("groups", "ep")),
    )
    out_specs = (P(("groups", "ep"), None), P(("groups", "ep"), None, None))
    return jax.shard_map(body, mesh=mesh, in_specs=in_specs, out_specs=out_specs, check_vma=False)
```

```python
import functools

import jax
import jax.numpy as jnp
from jax import lax
from jax.experimental import pallas as pl
from jax.experimental.pallas import tpu as pltpu
from jax.sharding import PartitionSpec as P

SPLIT = 4
NOPE = 512

softmax_scale = 192.0 ** (-0.5)


def attention(queries, latent_cache, lengths):
    scores = (
        jnp.einsum("rhc,rlc->rhl", queries, latent_cache, preferred_element_type=jnp.float32)
        * softmax_scale
    )
    positions = jnp.arange(latent_cache.shape[1], dtype=jnp.int32)
    valid_mask = positions[None, None, :] < lengths[:, None, None]
    scores = jnp.where(valid_mask, scores, -1e30)
    highest = jnp.max(scores, axis=-1, keepdims=True)
    expons = jnp.where(valid_mask, jnp.exp(scores - highest), 0.0)
    weights = (expons / jnp.sum(expons, axis=-1, keepdims=True)).astype(jnp.bfloat16)
    return jnp.einsum(
        "rhl,rlc->rhc", weights, latent_cache[:, :, :NOPE], preferred_element_type=jnp.float32
    ).astype(jnp.bfloat16)


def permutation(devices, far, near, swap_x, swap_core):
    outer_size = devices // 8
    pairs = []
    for source in range(devices):
        outer, inner, x, core = source // 8, source // 4 % 2, source // 2 % 2, source % 2
        target = ((outer + far) % outer_size * 2 + (inner ^ near)) * 4 + (x ^ swap_x) * 2 + (core ^ swap_core)
        pairs.append((source, target))
    return pairs


def after(array, *first):
    return lax.optimization_barrier((array,) + first)[0]


def expert_kernel(number, counts, parts, *refs):
    blocks, weights, outs = refs[:number], refs[number : number + 6], refs[number + 6 : -5]
    wide, tall, total, hidden, arrived = refs[-5:]
    model_width, width = weights[0].shape
    part_width = model_width // parts
    spans = [slice(p * part_width, (p + 1) * part_width) for p in range(parts)]
    wide_copies = [
        [
            pltpu.make_async_copy(weights[i].at[span], wide.at[i, span], arrived.at[p * 6 + i])
            for i in range(4)
        ]
        for p, span in enumerate(spans)
    ]
    tall_copies = [
        [
            pltpu.make_async_copy(
                weights[4 + i].at[:, span], tall.at[i, :, span], arrived.at[p * 6 + 4 + i]
            )
            for i in range(2)
        ]
        for p, span in enumerate(spans)
    ]
    for copies in wide_copies + tall_copies:
        for copy in copies:
            copy.start()
    for p, span in enumerate(spans):
        rows = jnp.concatenate([b[:, span] for b in blocks], axis=0)
        for i in range(4):
            wide_copies[p][i].wait()
            product = jnp.dot(rows, wide[i, span], preferred_element_type=jnp.float32)
            columns = slice(i * width, (i + 1) * width)
            total[:, columns] = product if p == 0 else total[:, columns] + product
    gate, up = total[:, : 2 * width], total[:, 2 * width :]
    hidden[...] = (gate / (1.0 + jnp.exp(-gate)) * up).astype(jnp.bfloat16)
    piece = part_width // 4
    for p in range(parts):
        for copy in tall_copies[p]:
            copy.wait()
        for q in range(4):
            columns = slice(p * part_width + q * piece, p * part_width + (q + 1) * piece)
            part = jnp.dot(
                hidden[:, :width], tall[0, :, columns], preferred_element_type=jnp.float32
            )
            part += jnp.dot(
                hidden[:, width:], tall[1, :, columns], preferred_element_type=jnp.float32
            )
            part = part.astype(jnp.bfloat16)
            at = 0
            for count, out in zip(counts, outs):
                out[:, columns] = part[at : at + count]
                at += count


def expert(blocks, counts, gates, ups, downs):
    model_width, width = gates[0].shape
    slots, parts = sum(counts), 2
    return pl.pallas_call(
        functools.partial(expert_kernel, len(blocks), counts, parts),
        in_specs=[pl.BlockSpec(memory_space=pltpu.VMEM)] * len(blocks)
        + [pl.BlockSpec(memory_space=pl.ANY)] * 6,
        out_specs=[pl.BlockSpec(memory_space=pltpu.VMEM)] * len(counts),
        out_shape=[jax.ShapeDtypeStruct((c, model_width), jnp.bfloat16) for c in counts],
        scratch_shapes=[
            pltpu.VMEM((4, model_width, width), jnp.bfloat16),
            pltpu.VMEM((2, width, model_width), jnp.bfloat16),
            pltpu.VMEM((slots, 4 * width), jnp.float32),
            pltpu.VMEM((slots, 2 * width), jnp.bfloat16),
            pltpu.SemaphoreType.DMA((6 * parts,)),
        ],
        compiler_params=pltpu.CompilerParams(vmem_limit_bytes=60 * 1024 * 1024),
        cost_estimate=pl.CostEstimate(
            flops=12 * slots * model_width * width,
            bytes_accessed=12 * model_width * width + 4 * slots * model_width,
            transcendentals=2 * slots * width,
        ),
    )(*blocks, *gates, *ups, *downs)


def combine_kernel(number, start, *refs):
    blocks, (places, shares), out = refs[:number], refs[number : number + 2], refs[-1]
    model_width = out.shape[1]
    piece = model_width // 7
    for lo in range(0, model_width, piece):
        columns = slice(lo, lo + piece)
        rows = jnp.concatenate([b[:, columns] for b in blocks], axis=0)
        total = refs[number + 2][:, columns] if start else 0.0
        for k in range(shares.shape[1]):
            picked = jnp.dot(places[k], rows, preferred_element_type=jnp.float32)
            total = total + picked * shares[:, k : k + 1]
        out[:, columns] = total.astype(out.dtype)


def combine(blocks, places, shares, dtype, *start):
    return pl.pallas_call(
        functools.partial(combine_kernel, len(blocks), bool(start)),
        out_shape=jax.ShapeDtypeStruct((shares.shape[0], blocks[0].shape[1]), dtype),
    )(*blocks, places, shares, *start)


def body(
    moe_rows,
    routes,
    gate_weights,
    gate_weight,
    up_weight,
    down_weight,
    queries,
    latent_cache,
    lengths,
):
    devices = lax.axis_size("ep")
    experts = devices // SPLIT
    outer_size = experts // 2
    row_count, model_width = moe_rows.shape
    top_count = routes.shape[1]
    capacity = 2 * row_count * top_count * SPLIT // devices
    me = lax.axis_index("ep")
    outer, inner = me // 8, me // 4 % 2

    def send(array, far=0, near=0, swap_x=0, swap_core=0):
        return lax.ppermute(array, "ep", permutation(devices, far, near, swap_x, swap_core))

    flat_routes = routes.reshape(-1)
    relative = (flat_routes // 2 - outer + outer_size) % outer_size * 2 + ((flat_routes % 2) ^ inner)
    onehot = (relative[:, None] == jnp.arange(experts, dtype=jnp.int32)[None, :]).astype(jnp.int32)
    earlier = jnp.cumsum(onehot, axis=0) - onehot
    slot_ids = jnp.sum(earlier * onehot, axis=1)
    targets = (relative * capacity + slot_ids).reshape(row_count, top_count)
    slots = jnp.arange(experts * capacity, dtype=jnp.int32)[None, None, :]
    spread = jnp.any(targets[:, :, None] == slots, axis=1).astype(jnp.bfloat16)
    outgoing = jnp.einsum(
        "rp,rd->pd", spread, moe_rows, preferred_element_type=jnp.float32
    ).astype(jnp.bfloat16)

    def outgoing_block(far, near):
        at = (far * 2 + near) * capacity
        return outgoing[at : at + capacity]

    close = sorted({1, outer_size - 1} - {0})
    rest = [(f, n) for f in range(2, outer_size - 1) for n in range(2)]
    near = [(close[0], n) for n in range(2)]
    last = [(close[1], n) for n in range(2)]
    rows, crossed = {(0, 0): outgoing_block(0, 0)}, {}

    def step(key, *first):
        rows[key] = send(after(outgoing_block(*key), *first), *key)

    def cross(keys, *first):
        together = jnp.concatenate([rows[key] for key in keys], axis=0)
        crossed[keys[0]] = send(after(together, *first) if first else together, swap_x=1)

    gate_other = send(gate_weight, swap_core=1)
    up_other = send(up_weight, swap_core=1)
    for key in rest:
        step(key)
    beside = send(outgoing[: 2 * capacity], swap_x=1)
    begun = [gate_other, up_other, beside] + [rows[key] for key in rest]
    cross(rest, *begun)
    pair = jnp.concatenate([outgoing_block(0, 1), beside[capacity:]], axis=0)
    pair = send(after(pair, *begun), near=1)
    for key in near:
        step(key, *begun)
    down_other = send(after(down_weight, *begun), swap_core=1)
    begun = [crossed[rest[0]], down_other] + [rows[key] for key in near]
    for key in last:
        step(key, *begun)
    cross(near, *begun)

    mine, theirs = {}, {}

    def run(groups, returns, *others):
        keys = [key for group in groups for key in group]
        blocks = [rows[key] for key in keys] + [crossed[group[0]] for group in groups]
        counts = (capacity,) * len(keys) + tuple(capacity * len(group) for group in returns)
        outs = expert(
            blocks + list(others),
            counts + tuple(other.shape[0] for other in others),
            (gate_weight, gate_other),
            (up_weight, up_other),
            (down_weight, down_other),
        )
        mine.update(zip(keys, outs))
        theirs.update(zip([group[0] for group in returns], outs[len(keys) :]))
        return outs[len(counts) :]

    back, totals, returned = {}, {}, {}

    def give_back(keys, *first):
        back[keys[0]] = send(after(theirs[keys[0]], *first), swap_x=1)

    def add(one, other):
        return (one.astype(jnp.float32) + other.astype(jnp.float32)).astype(jnp.bfloat16)

    def finish(keys, *first):
        came = after(back[keys[0]], *first)
        for i, key in enumerate(keys):
            totals[key] = add(mine[key], came[i * capacity : (i + 1) * capacity])
            returned[key] = send(totals[key], -key[0], key[1])

    run([rest], [rest])
    give_back(rest)
    cross(last, theirs[rest[0]])
    own_mine, own_theirs, own_pair = run(
        [near], [near], rows[0, 0], beside[:capacity], pair
    )
    give_back(near)
    finish(rest, mine[near[0]])
    own_pair = send(after(own_pair, *(totals[key] for key in rest)), near=1)
    singles = [[key] for key in last]
    run([last], singles)
    for keys in singles:
        give_back(keys, back[near[0]], *(returned[key] for key in rest))
    own_back = jnp.concatenate([own_theirs, own_pair[capacity:]], axis=0)
    own_back = send(after(own_back, back[last[0]]), swap_x=1)
    for keys in [near] + singles:
        finish(keys)
    own_back = after(own_back, returned[near[0]])
    returned[0, 0] = add(own_mine, own_back[:capacity])
    returned[0, 1] = add(own_pair[:capacity], own_back[capacity:])

    places = after(targets, theirs[near[0]])[:, :, None] == slots
    places = places.astype(jnp.bfloat16).transpose(1, 0, 2)
    shares = after(gate_weights, theirs[near[0]])

    def gather(keys, dtype, *start):
        columns = [
            places[:, :, (f * 2 + n) * capacity : (f * 2 + n + 1) * capacity] for f, n in keys
        ]
        return combine(
            [returned[key] for key in keys],
            jnp.concatenate(columns, axis=2),
            shares,
            dtype,
            *start,
        )

    most = gather(rest + near, jnp.float32)
    moe_out = gather([(0, 0), (0, 1)] + last, jnp.bfloat16, most)
    attn_out = attention(after(queries, back[last[0]]), latent_cache, lengths)
    return (moe_out, attn_out)


def solution(mesh):
    in_specs = (
        P(("groups", "ep"), None),
        P(("groups", "ep"), None),
        P(("groups", "ep"), None),
        P(None, "ep"),
        P(None, "ep"),
        P("ep", None),
        P(("groups", "ep"), None, None),
        P(("groups", "ep"), None, None),
        P(("groups", "ep")),
    )
    out_specs = (P(("groups", "ep"), None), P(("groups", "ep"), None, None))
    return jax.shard_map(body, mesh=mesh, in_specs=in_specs, out_specs=out_specs, check_vma=False)
```

```python
import functools

import jax
import jax.numpy as jnp
from jax import lax
from jax.experimental import pallas as pl
from jax.experimental.pallas import tpu as pltpu
from jax.sharding import PartitionSpec as P

SPLIT = 4
NOPE = 512

softmax_scale = 192.0 ** (-0.5)


def attention(queries, latent_cache, lengths):
    scores = (
        jnp.einsum("rhc,rlc->rhl", queries, latent_cache, preferred_element_type=jnp.float32)
        * softmax_scale
    )
    positions = jnp.arange(latent_cache.shape[1], dtype=jnp.int32)
    valid_mask = positions[None, None, :] < lengths[:, None, None]
    scores = jnp.where(valid_mask, scores, -1e30)
    highest = jnp.max(scores, axis=-1, keepdims=True)
    expons = jnp.where(valid_mask, jnp.exp(scores - highest), 0.0)
    weights = (expons / jnp.sum(expons, axis=-1, keepdims=True)).astype(jnp.bfloat16)
    return jnp.einsum(
        "rhl,rlc->rhc", weights, latent_cache[:, :, :NOPE], preferred_element_type=jnp.float32
    ).astype(jnp.bfloat16)


def permutation(devices, far, near, swap_x, swap_core):
    outer_size = devices // 8
    pairs = []
    for source in range(devices):
        outer, inner, x, core = source // 8, source // 4 % 2, source // 2 % 2, source % 2
        target = ((outer + far) % outer_size * 2 + (inner ^ near)) * 4 + (x ^ swap_x) * 2 + (core ^ swap_core)
        pairs.append((source, target))
    return pairs


def after(array, *first):
    return lax.optimization_barrier((array,) + first)[0]


def expert_kernel(number, counts, parts, resident, *refs):
    blocks, weights, outs = refs[:number], refs[number : number + 6], refs[number + 6 : -5]
    wide, tall, total, hidden, arrived = refs[-5:]
    model_width, width = weights[0].shape
    part_width = model_width // parts
    spans = [slice(p * part_width, (p + 1) * part_width) for p in range(parts)]
    fetched = [i for i in range(4) if i not in resident]
    wide_copies = [
        {
            i: pltpu.make_async_copy(
                weights[i].at[span], wide.at[at, span], arrived.at[p * 6 + at]
            )
            for at, i in enumerate(fetched)
        }
        for p, span in enumerate(spans)
    ]
    tall_copies = [
        [
            pltpu.make_async_copy(
                weights[4 + i].at[:, span], tall.at[i, :, span], arrived.at[p * 6 + 4 + i]
            )
            for i in range(2)
        ]
        for p, span in enumerate(spans)
    ]
    for copies in [list(c.values()) for c in wide_copies] + tall_copies:
        for copy in copies:
            copy.start()
    order = [(p, i) for p in range(parts) for i in resident]
    order += [(p, i) for p in range(parts) for i in fetched]
    for p, i in order:
        span = spans[p]
        rows = jnp.concatenate([b[:, span] for b in blocks], axis=0)
        if i in resident:
            weight = weights[i][span]
        else:
            wide_copies[p][i].wait()
            weight = wide[fetched.index(i), span]
        product = jnp.dot(rows, weight, preferred_element_type=jnp.float32)
        columns = slice(i * width, (i + 1) * width)
        total[:, columns] = product if p == 0 else total[:, columns] + product
    gate, up = total[:, : 2 * width], total[:, 2 * width :]
    hidden[...] = (gate / (1.0 + jnp.exp(-gate)) * up).astype(jnp.bfloat16)
    piece = part_width // 4
    for p in range(parts):
        for copy in tall_copies[p]:
            copy.wait()
        for q in range(4):
            columns = slice(p * part_width + q * piece, p * part_width + (q + 1) * piece)
            part = jnp.dot(
                hidden[:, :width], tall[0, :, columns], preferred_element_type=jnp.float32
            )
            part += jnp.dot(
                hidden[:, width:], tall[1, :, columns], preferred_element_type=jnp.float32
            )
            part = part.astype(jnp.bfloat16)
            at = 0
            for count, out in zip(counts, outs):
                out[:, columns] = part[at : at + count]
                at += count


def expert(blocks, counts, gates, ups, downs, resident=()):
    model_width, width = gates[0].shape
    slots, parts = sum(counts), 2
    return pl.pallas_call(
        functools.partial(expert_kernel, len(blocks), counts, parts, resident),
        in_specs=[pl.BlockSpec(memory_space=pltpu.VMEM)] * len(blocks)
        + [
            pl.BlockSpec(memory_space=pltpu.VMEM if i in resident else pl.ANY) for i in range(6)
        ],
        out_specs=[pl.BlockSpec(memory_space=pltpu.VMEM)] * len(counts),
        out_shape=[jax.ShapeDtypeStruct((c, model_width), jnp.bfloat16) for c in counts],
        scratch_shapes=[
            pltpu.VMEM((4 - len(resident), model_width, width), jnp.bfloat16),
            pltpu.VMEM((2, width, model_width), jnp.bfloat16),
            pltpu.VMEM((slots, 4 * width), jnp.float32),
            pltpu.VMEM((slots, 2 * width), jnp.bfloat16),
            pltpu.SemaphoreType.DMA((6 * parts,)),
        ],
        compiler_params=pltpu.CompilerParams(vmem_limit_bytes=(40 if resident else 60) * 1024 * 1024),
        cost_estimate=pl.CostEstimate(
            flops=12 * slots * model_width * width,
            bytes_accessed=12 * model_width * width + 4 * slots * model_width,
            transcendentals=2 * slots * width,
        ),
    )(*blocks, *gates, *ups, *downs)


def combine_kernel(number, start, *refs):
    blocks, (places, shares), out = refs[:number], refs[number : number + 2], refs[-1]
    model_width = out.shape[1]
    piece = model_width // 7
    for lo in range(0, model_width, piece):
        columns = slice(lo, lo + piece)
        rows = jnp.concatenate([b[:, columns] for b in blocks], axis=0)
        total = refs[number + 2][:, columns] if start else 0.0
        for k in range(shares.shape[1]):
            picked = jnp.dot(places[k], rows, preferred_element_type=jnp.float32)
            total = total + picked * shares[:, k : k + 1]
        out[:, columns] = total.astype(out.dtype)


def combine(blocks, places, shares, dtype, *start):
    return pl.pallas_call(
        functools.partial(combine_kernel, len(blocks), bool(start)),
        out_shape=jax.ShapeDtypeStruct((shares.shape[0], blocks[0].shape[1]), dtype),
    )(*blocks, places, shares, *start)


def body(
    moe_rows,
    routes,
    gate_weights,
    gate_weight,
    up_weight,
    down_weight,
    queries,
    latent_cache,
    lengths,
):
    devices = lax.axis_size("ep")
    experts = devices // SPLIT
    outer_size = experts // 2
    row_count, model_width = moe_rows.shape
    top_count = routes.shape[1]
    capacity = 2 * row_count * top_count * SPLIT // devices
    me = lax.axis_index("ep")
    outer, inner = me // 8, me // 4 % 2

    def send(array, far=0, near=0, swap_x=0, swap_core=0):
        return lax.ppermute(array, "ep", permutation(devices, far, near, swap_x, swap_core))

    flat_routes = routes.reshape(-1)
    relative = (flat_routes // 2 - outer + outer_size) % outer_size * 2 + ((flat_routes % 2) ^ inner)
    onehot = (relative[:, None] == jnp.arange(experts, dtype=jnp.int32)[None, :]).astype(jnp.int32)
    earlier = jnp.cumsum(onehot, axis=0) - onehot
    slot_ids = jnp.sum(earlier * onehot, axis=1)
    targets = (relative * capacity + slot_ids).reshape(row_count, top_count)
    slots = jnp.arange(experts * capacity, dtype=jnp.int32)[None, None, :]
    spread = jnp.any(targets[:, :, None] == slots, axis=1).astype(jnp.bfloat16)
    outgoing = jnp.einsum(
        "rp,rd->pd", spread, moe_rows, preferred_element_type=jnp.float32
    ).astype(jnp.bfloat16)

    def outgoing_block(far, near):
        at = (far * 2 + near) * capacity
        return outgoing[at : at + capacity]

    close = sorted({1, outer_size - 1} - {0})
    rest = [(f, n) for f in range(2, outer_size - 1) for n in range(2)]
    near = [(close[0], n) for n in range(2)]
    last = [(close[1], n) for n in range(2)]
    rows, crossed = {(0, 0): outgoing_block(0, 0)}, {}

    def step(key, *first):
        rows[key] = send(after(outgoing_block(*key), *first), *key)

    def cross(keys, *first):
        together = jnp.concatenate([rows[key] for key in keys], axis=0)
        crossed[keys[0]] = send(after(together, *first) if first else together, swap_x=1)

    gate_other = send(gate_weight, swap_core=1)
    up_other = send(up_weight, swap_core=1)
    for key in rest:
        step(key)
    beside = send(outgoing[: 2 * capacity], swap_x=1)
    begun = [gate_other, up_other, beside] + [rows[key] for key in rest]
    cross(rest, *begun)
    pair = jnp.concatenate([outgoing_block(0, 1), beside[capacity:]], axis=0)
    pair = send(after(pair, *begun), near=1)
    for key in near:
        step(key, *begun)
    down_other = send(after(down_weight, *begun), swap_core=1)
    begun = [crossed[rest[0]], down_other] + [rows[key] for key in near]
    for key in last:
        step(key, *begun)
    cross(near, *begun)

    mine, theirs = {}, {}

    def run(groups, returns, *others, resident=()):
        keys = [key for group in groups for key in group]
        blocks = [rows[key] for key in keys] + [crossed[group[0]] for group in groups]
        counts = (capacity,) * len(keys) + tuple(capacity * len(group) for group in returns)
        outs = expert(
            blocks + list(others),
            counts + tuple(other.shape[0] for other in others),
            (gate_weight, gate_other),
            (up_weight, up_other),
            (down_weight, down_other),
            resident,
        )
        mine.update(zip(keys, outs))
        theirs.update(zip([group[0] for group in returns], outs[len(keys) :]))
        return outs[len(counts) :]

    back, totals, returned = {}, {}, {}

    def give_back(keys, *first):
        back[keys[0]] = send(after(theirs[keys[0]], *first), swap_x=1)

    def add(one, other):
        return (one.astype(jnp.float32) + other.astype(jnp.float32)).astype(jnp.bfloat16)

    def finish(keys, *first):
        came = after(back[keys[0]], *first)
        for i, key in enumerate(keys):
            totals[key] = add(mine[key], came[i * capacity : (i + 1) * capacity])
            returned[key] = send(totals[key], -key[0], key[1])

    run([rest], [rest], resident=(0, 2))
    give_back(rest)
    cross(last, theirs[rest[0]])
    own_mine, own_theirs, own_pair = run(
        [near], [near], rows[0, 0], beside[:capacity], pair
    )
    give_back(near)
    finish(rest, mine[near[0]])
    own_pair = send(after(own_pair, *(totals[key] for key in rest)), near=1)
    singles = [[key] for key in last]
    run([last], singles)
    for keys in singles:
        give_back(keys, back[near[0]], *(returned[key] for key in rest))
    own_back = jnp.concatenate([own_theirs, own_pair[capacity:]], axis=0)
    own_back = send(after(own_back, back[last[0]]), swap_x=1)
    for keys in [near] + singles:
        finish(keys)
    own_back = after(own_back, returned[near[0]])
    returned[0, 0] = add(own_mine, own_back[:capacity])
    returned[0, 1] = add(own_pair[:capacity], own_back[capacity:])

    places = after(targets, theirs[near[0]])[:, :, None] == slots
    places = places.astype(jnp.bfloat16).transpose(1, 0, 2)
    shares = after(gate_weights, theirs[near[0]])

    def gather(keys, dtype, *start):
        columns = [
            places[:, :, (f * 2 + n) * capacity : (f * 2 + n + 1) * capacity] for f, n in keys
        ]
        return combine(
            [returned[key] for key in keys],
            jnp.concatenate(columns, axis=2),
            shares,
            dtype,
            *start,
        )

    most = gather(rest + near, jnp.float32)
    moe_out = gather([(0, 0), (0, 1)] + last, jnp.bfloat16, most)
    attn_out = attention(after(queries, back[last[0]]), latent_cache, lengths)
    return (moe_out, attn_out)


def solution(mesh):
    in_specs = (
        P(("groups", "ep"), None),
        P(("groups", "ep"), None),
        P(("groups", "ep"), None),
        P(None, "ep"),
        P(None, "ep"),
        P("ep", None),
        P(("groups", "ep"), None, None),
        P(("groups", "ep"), None, None),
        P(("groups", "ep")),
    )
    out_specs = (P(("groups", "ep"), None), P(("groups", "ep"), None, None))
    return jax.shard_map(body, mesh=mesh, in_specs=in_specs, out_specs=out_specs, check_vma=False)
```

```python
import functools

import jax
import jax.numpy as jnp
from jax import lax
from jax.experimental import pallas as pl
from jax.experimental.pallas import tpu as pltpu
from jax.sharding import PartitionSpec as P

SPLIT = 4
NOPE = 512

softmax_scale = 192.0 ** (-0.5)


def attention(queries, latent_cache, lengths):
    scores = (
        jnp.einsum("rhc,rlc->rhl", queries, latent_cache, preferred_element_type=jnp.float32)
        * softmax_scale
    )
    positions = jnp.arange(latent_cache.shape[1], dtype=jnp.int32)
    valid_mask = positions[None, None, :] < lengths[:, None, None]
    scores = jnp.where(valid_mask, scores, -1e30)
    highest = jnp.max(scores, axis=-1, keepdims=True)
    expons = jnp.where(valid_mask, jnp.exp(scores - highest), 0.0)
    weights = (expons / jnp.sum(expons, axis=-1, keepdims=True)).astype(jnp.bfloat16)
    return jnp.einsum(
        "rhl,rlc->rhc", weights, latent_cache[:, :, :NOPE], preferred_element_type=jnp.float32
    ).astype(jnp.bfloat16)


def permutation(devices, far, near, swap_x, swap_core):
    outer_size = devices // 8
    pairs = []
    for source in range(devices):
        outer, inner, x, core = source // 8, source // 4 % 2, source // 2 % 2, source % 2
        target = ((outer + far) % outer_size * 2 + (inner ^ near)) * 4 + (x ^ swap_x) * 2 + (core ^ swap_core)
        pairs.append((source, target))
    return pairs


def after(array, *first):
    return lax.optimization_barrier((array,) + first)[0]


def expert_kernel(number, counts, parts, resident, *refs):
    blocks, weights, outs = refs[:number], refs[number : number + 6], refs[number + 6 : -5]
    wide, tall, total, hidden, arrived = refs[-5:]
    model_width, width = weights[0].shape
    part_width = model_width // parts
    spans = [slice(p * part_width, (p + 1) * part_width) for p in range(parts)]
    fetched = [i for i in range(4) if i not in resident]
    wide_copies = [
        {
            i: pltpu.make_async_copy(
                weights[i].at[span], wide.at[at, span], arrived.at[p * 6 + at]
            )
            for at, i in enumerate(fetched)
        }
        for p, span in enumerate(spans)
    ]
    tall_copies = [
        [
            pltpu.make_async_copy(
                weights[4 + i].at[:, span], tall.at[i, :, span], arrived.at[p * 6 + 4 + i]
            )
            for i in range(2)
        ]
        for p, span in enumerate(spans)
    ]
    for copies in [list(c.values()) for c in wide_copies] + tall_copies:
        for copy in copies:
            copy.start()
    order = [(p, i) for p in range(parts) for i in resident]
    order += [(p, i) for p in range(parts) for i in fetched]
    for p, i in order:
        span = spans[p]
        rows = jnp.concatenate([b[:, span] for b in blocks], axis=0)
        if i in resident:
            weight = weights[i][span]
        else:
            wide_copies[p][i].wait()
            weight = wide[fetched.index(i), span]
        product = jnp.dot(rows, weight, preferred_element_type=jnp.float32)
        columns = slice(i * width, (i + 1) * width)
        total[:, columns] = product if p == 0 else total[:, columns] + product
    gate, up = total[:, : 2 * width], total[:, 2 * width :]
    hidden[...] = (gate / (1.0 + jnp.exp(-gate)) * up).astype(jnp.bfloat16)
    piece = part_width // 4
    for p in range(parts):
        for copy in tall_copies[p]:
            copy.wait()
        for q in range(4):
            columns = slice(p * part_width + q * piece, p * part_width + (q + 1) * piece)
            part = jnp.dot(
                hidden[:, :width], tall[0, :, columns], preferred_element_type=jnp.float32
            )
            part += jnp.dot(
                hidden[:, width:], tall[1, :, columns], preferred_element_type=jnp.float32
            )
            part = part.astype(jnp.bfloat16)
            at = 0
            for count, out in zip(counts, outs):
                out[:, columns] = part[at : at + count]
                at += count


def expert(blocks, counts, gates, ups, downs, resident=()):
    model_width, width = gates[0].shape
    slots, parts = sum(counts), 2
    return pl.pallas_call(
        functools.partial(expert_kernel, len(blocks), counts, parts, resident),
        in_specs=[pl.BlockSpec(memory_space=pltpu.VMEM)] * len(blocks)
        + [
            pl.BlockSpec(memory_space=pltpu.VMEM if i in resident else pl.ANY) for i in range(6)
        ],
        out_specs=[pl.BlockSpec(memory_space=pltpu.VMEM)] * len(counts),
        out_shape=[jax.ShapeDtypeStruct((c, model_width), jnp.bfloat16) for c in counts],
        scratch_shapes=[
            pltpu.VMEM((4 - len(resident), model_width, width), jnp.bfloat16),
            pltpu.VMEM((2, width, model_width), jnp.bfloat16),
            pltpu.VMEM((slots, 4 * width), jnp.float32),
            pltpu.VMEM((slots, 2 * width), jnp.bfloat16),
            pltpu.SemaphoreType.DMA((6 * parts,)),
        ],
        compiler_params=pltpu.CompilerParams(vmem_limit_bytes=(40 if resident else 60) * 1024 * 1024),
        cost_estimate=pl.CostEstimate(
            flops=12 * slots * model_width * width,
            bytes_accessed=12 * model_width * width + 4 * slots * model_width,
            transcendentals=2 * slots * width,
        ),
    )(*blocks, *gates, *ups, *downs)


def combine_kernel(number, start, *refs):
    blocks, (places, shares), out = refs[:number], refs[number : number + 2], refs[-1]
    model_width = out.shape[1]
    piece = model_width // 7
    for lo in range(0, model_width, piece):
        columns = slice(lo, lo + piece)
        rows = jnp.concatenate([b[:, columns] for b in blocks], axis=0)
        total = refs[number + 2][:, columns] if start else 0.0
        for k in range(shares.shape[1]):
            picked = jnp.dot(places[k], rows, preferred_element_type=jnp.float32)
            total = total + picked * shares[:, k : k + 1]
        out[:, columns] = total.astype(out.dtype)


def combine(blocks, places, shares, dtype, *start):
    return pl.pallas_call(
        functools.partial(combine_kernel, len(blocks), bool(start)),
        out_shape=jax.ShapeDtypeStruct((shares.shape[0], blocks[0].shape[1]), dtype),
    )(*blocks, places, shares, *start)


def body(
    moe_rows,
    routes,
    gate_weights,
    gate_weight,
    up_weight,
    down_weight,
    queries,
    latent_cache,
    lengths,
):
    devices = lax.axis_size("ep")
    experts = devices // SPLIT
    outer_size = experts // 2
    row_count, model_width = moe_rows.shape
    top_count = routes.shape[1]
    capacity = 2 * row_count * top_count * SPLIT // devices
    me = lax.axis_index("ep")
    outer, inner = me // 8, me // 4 % 2

    def send(array, far=0, near=0, swap_x=0, swap_core=0):
        return lax.ppermute(array, "ep", permutation(devices, far, near, swap_x, swap_core))

    flat_routes = routes.reshape(-1)
    relative = (flat_routes // 2 - outer + outer_size) % outer_size * 2 + ((flat_routes % 2) ^ inner)
    onehot = (relative[:, None] == jnp.arange(experts, dtype=jnp.int32)[None, :]).astype(jnp.int32)
    earlier = jnp.cumsum(onehot, axis=0) - onehot
    slot_ids = jnp.sum(earlier * onehot, axis=1)
    targets = (relative * capacity + slot_ids).reshape(row_count, top_count)
    slots = jnp.arange(experts * capacity, dtype=jnp.int32)[None, None, :]
    spread = jnp.any(targets[:, :, None] == slots, axis=1).astype(jnp.bfloat16)
    outgoing = jnp.einsum(
        "rp,rd->pd", spread, moe_rows, preferred_element_type=jnp.float32
    ).astype(jnp.bfloat16)

    def outgoing_block(far, near):
        at = (far * 2 + near) * capacity
        return outgoing[at : at + capacity]

    close = sorted({1, outer_size - 1} - {0})
    rest = [(f, n) for f in range(2, outer_size - 1) for n in range(2)]
    near = [(close[0], n) for n in range(2)]
    last = [(close[1], n) for n in range(2)]
    rows, crossed = {(0, 0): outgoing_block(0, 0)}, {}

    def step(key, *first):
        rows[key] = send(after(outgoing_block(*key), *first), *key)

    def cross(keys, *first):
        together = jnp.concatenate([rows[key] for key in keys], axis=0)
        crossed[keys[0]] = send(after(together, *first) if first else together, swap_x=1)

    gate_other = send(gate_weight, swap_core=1)
    up_other = send(up_weight, swap_core=1)
    for key in rest:
        step(key)
    beside = send(outgoing[: 2 * capacity], swap_x=1)
    begun = [gate_other, up_other, beside] + [rows[key] for key in rest]
    cross(rest, *begun)
    pair = jnp.concatenate([outgoing_block(0, 1), beside[capacity:]], axis=0)
    pair = send(after(pair, *begun), near=1)
    for key in near:
        step(key, *begun)
    down_other = send(after(down_weight, *begun), swap_core=1)
    begun = [crossed[rest[0]], down_other] + [rows[key] for key in near]
    for key in last:
        step(key, *begun)
    cross(near, *begun)

    mine, theirs = {}, {}

    def run(groups, returns, *others, resident=()):
        keys = [key for group in groups for key in group]
        blocks = [rows[key] for key in keys] + [crossed[group[0]] for group in groups]
        counts = (capacity,) * len(keys) + tuple(capacity * len(group) for group in returns)
        outs = expert(
            blocks + list(others),
            counts + tuple(other.shape[0] for other in others),
            (gate_weight, gate_other),
            (up_weight, up_other),
            (down_weight, down_other),
            resident,
        )
        mine.update(zip(keys, outs))
        theirs.update(zip([group[0] for group in returns], outs[len(keys) :]))
        return outs[len(counts) :]

    back, totals, returned = {}, {}, {}

    def give_back(keys, *first):
        back[keys[0]] = send(after(theirs[keys[0]], *first), swap_x=1)

    def add(one, other):
        return (one.astype(jnp.float32) + other.astype(jnp.float32)).astype(jnp.bfloat16)

    def finish(keys, *first):
        came = after(back[keys[0]], *first)
        for i, key in enumerate(keys):
            totals[key] = add(mine[key], came[i * capacity : (i + 1) * capacity])
            returned[key] = send(totals[key], -key[0], key[1])

    run([rest], [rest], resident=(0, 2))
    give_back(rest)
    cross(last, theirs[rest[0]])
    own_mine, own_theirs, own_pair = run(
        [near], [near], rows[0, 0], beside[:capacity], pair, resident=(0, 2)
    )
    give_back(near)
    finish(rest, mine[near[0]])
    own_pair = send(after(own_pair, *(totals[key] for key in rest)), near=1)
    singles = [[key] for key in last]
    run([last], singles)
    for keys in singles:
        give_back(keys, back[near[0]], *(returned[key] for key in rest))
    own_back = jnp.concatenate([own_theirs, own_pair[capacity:]], axis=0)
    own_back = send(after(own_back, back[last[0]]), swap_x=1)
    for keys in [near] + singles:
        finish(keys)
    own_back = after(own_back, returned[near[0]])
    returned[0, 0] = add(own_mine, own_back[:capacity])
    returned[0, 1] = add(own_pair[:capacity], own_back[capacity:])

    places = after(targets, theirs[near[0]])[:, :, None] == slots
    places = places.astype(jnp.bfloat16).transpose(1, 0, 2)
    shares = after(gate_weights, theirs[near[0]])

    def gather(keys, dtype, *start):
        columns = [
            places[:, :, (f * 2 + n) * capacity : (f * 2 + n + 1) * capacity] for f, n in keys
        ]
        return combine(
            [returned[key] for key in keys],
            jnp.concatenate(columns, axis=2),
            shares,
            dtype,
            *start,
        )

    most = gather(rest + near, jnp.float32)
    moe_out = gather([(0, 0), (0, 1)] + last, jnp.bfloat16, most)
    attn_out = attention(after(queries, back[last[0]]), latent_cache, lengths)
    return (moe_out, attn_out)


def solution(mesh):
    in_specs = (
        P(("groups", "ep"), None),
        P(("groups", "ep"), None),
        P(("groups", "ep"), None),
        P(None, "ep"),
        P(None, "ep"),
        P("ep", None),
        P(("groups", "ep"), None, None),
        P(("groups", "ep"), None, None),
        P(("groups", "ep")),
    )
    out_specs = (P(("groups", "ep"), None), P(("groups", "ep"), None, None))
    return jax.shard_map(body, mesh=mesh, in_specs=in_specs, out_specs=out_specs, check_vma=False)
```

```python
import functools

import jax
import jax.numpy as jnp
from jax import lax
from jax.experimental import pallas as pl
from jax.experimental.pallas import tpu as pltpu
from jax.sharding import PartitionSpec as P

SPLIT = 4
NOPE = 512

softmax_scale = 192.0 ** (-0.5)


def attention(queries, latent_cache, lengths):
    scores = (
        jnp.einsum("rhc,rlc->rhl", queries, latent_cache, preferred_element_type=jnp.float32)
        * softmax_scale
    )
    positions = jnp.arange(latent_cache.shape[1], dtype=jnp.int32)
    valid_mask = positions[None, None, :] < lengths[:, None, None]
    scores = jnp.where(valid_mask, scores, -1e30)
    highest = jnp.max(scores, axis=-1, keepdims=True)
    expons = jnp.where(valid_mask, jnp.exp(scores - highest), 0.0)
    weights = (expons / jnp.sum(expons, axis=-1, keepdims=True)).astype(jnp.bfloat16)
    return jnp.einsum(
        "rhl,rlc->rhc", weights, latent_cache[:, :, :NOPE], preferred_element_type=jnp.float32
    ).astype(jnp.bfloat16)


def permutation(devices, far, near, swap_x, swap_core):
    outer_size = devices // 8
    pairs = []
    for source in range(devices):
        outer, inner, x, core = source // 8, source // 4 % 2, source // 2 % 2, source % 2
        target = ((outer + far) % outer_size * 2 + (inner ^ near)) * 4 + (x ^ swap_x) * 2 + (core ^ swap_core)
        pairs.append((source, target))
    return pairs


def after(array, *first):
    return lax.optimization_barrier((array,) + first)[0]


def expert_kernel(number, counts, parts, resident, *refs):
    blocks, weights, outs = refs[:number], refs[number : number + 6], refs[number + 6 : -5]
    wide, tall, total, hidden, arrived = refs[-5:]
    model_width, width = weights[0].shape
    part_width = model_width // parts
    spans = [slice(p * part_width, (p + 1) * part_width) for p in range(parts)]
    fetched = [i for i in range(4) if i not in resident]
    wide_copies = [
        {
            i: pltpu.make_async_copy(
                weights[i].at[span], wide.at[at, span], arrived.at[p * 6 + at]
            )
            for at, i in enumerate(fetched)
        }
        for p, span in enumerate(spans)
    ]
    tall_copies = [
        [
            pltpu.make_async_copy(
                weights[4 + i].at[:, span], tall.at[i, :, span], arrived.at[p * 6 + 4 + i]
            )
            for i in range(2)
        ]
        for p, span in enumerate(spans)
    ]
    for copies in [list(c.values()) for c in wide_copies] + tall_copies:
        for copy in copies:
            copy.start()
    order = [(p, i) for p in range(parts) for i in resident]
    order += [(p, i) for p in range(parts) for i in fetched]
    for p, i in order:
        span = spans[p]
        rows = jnp.concatenate([b[:, span] for b in blocks], axis=0)
        if i in resident:
            weight = weights[i][span]
        else:
            wide_copies[p][i].wait()
            weight = wide[fetched.index(i), span]
        product = jnp.dot(rows, weight, preferred_element_type=jnp.float32)
        columns = slice(i * width, (i + 1) * width)
        total[:, columns] = product if p == 0 else total[:, columns] + product
    gate, up = total[:, : 2 * width], total[:, 2 * width :]
    hidden[...] = (gate / (1.0 + jnp.exp(-gate)) * up).astype(jnp.bfloat16)
    piece = part_width // 4
    for p in range(parts):
        for copy in tall_copies[p]:
            copy.wait()
        for q in range(4):
            columns = slice(p * part_width + q * piece, p * part_width + (q + 1) * piece)
            part = jnp.dot(
                hidden[:, :width], tall[0, :, columns], preferred_element_type=jnp.float32
            )
            part += jnp.dot(
                hidden[:, width:], tall[1, :, columns], preferred_element_type=jnp.float32
            )
            part = part.astype(jnp.bfloat16)
            at = 0
            for count, out in zip(counts, outs):
                out[:, columns] = part[at : at + count]
                at += count


def expert(blocks, counts, gates, ups, downs, resident=()):
    model_width, width = gates[0].shape
    slots, parts = sum(counts), 2
    return pl.pallas_call(
        functools.partial(expert_kernel, len(blocks), counts, parts, resident),
        in_specs=[pl.BlockSpec(memory_space=pltpu.VMEM)] * len(blocks)
        + [
            pl.BlockSpec(memory_space=pltpu.VMEM if i in resident else pl.ANY) for i in range(6)
        ],
        out_specs=[pl.BlockSpec(memory_space=pltpu.VMEM)] * len(counts),
        out_shape=[jax.ShapeDtypeStruct((c, model_width), jnp.bfloat16) for c in counts],
        scratch_shapes=[
            pltpu.VMEM((4 - len(resident), model_width, width), jnp.bfloat16),
            pltpu.VMEM((2, width, model_width), jnp.bfloat16),
            pltpu.VMEM((slots, 4 * width), jnp.float32),
            pltpu.VMEM((slots, 2 * width), jnp.bfloat16),
            pltpu.SemaphoreType.DMA((6 * parts,)),
        ],
        compiler_params=pltpu.CompilerParams(vmem_limit_bytes=(40 if resident else 60) * 1024 * 1024),
        cost_estimate=pl.CostEstimate(
            flops=12 * slots * model_width * width,
            bytes_accessed=12 * model_width * width + 4 * slots * model_width,
            transcendentals=2 * slots * width,
        ),
    )(*blocks, *gates, *ups, *downs)


def combine_kernel(number, start, *refs):
    blocks, (places, shares), out = refs[:number], refs[number : number + 2], refs[-1]
    model_width = out.shape[1]
    piece = model_width // 7
    for lo in range(0, model_width, piece):
        columns = slice(lo, lo + piece)
        rows = jnp.concatenate([b[:, columns] for b in blocks], axis=0)
        total = refs[number + 2][:, columns] if start else 0.0
        for k in range(shares.shape[1]):
            picked = jnp.dot(places[k], rows, preferred_element_type=jnp.float32)
            total = total + picked * shares[:, k : k + 1]
        out[:, columns] = total.astype(out.dtype)


def combine(blocks, places, shares, dtype, *start):
    return pl.pallas_call(
        functools.partial(combine_kernel, len(blocks), bool(start)),
        out_shape=jax.ShapeDtypeStruct((shares.shape[0], blocks[0].shape[1]), dtype),
    )(*blocks, places, shares, *start)


def pack_kernel(experts, capacity, routes, rows, *outs):
    me = lax.axis_index("ep")
    outer, inner, outer_size = me // 8, me // 4 % 2, experts // 2
    row_count, top_count = routes.shape
    model_width = rows.shape[1]
    number = lax.broadcasted_iota(jnp.int32, (row_count, experts), 1)
    named = []
    for k in range(top_count):
        route = routes[:, k : k + 1]
        far = route // 2 - outer
        far = jnp.where(far < 0, far + outer_size, far)
        named.append(far * 2 + ((route % 2) ^ inner))
    onehots = [(number == n).astype(jnp.float32) for n in named]
    shape = (row_count, row_count)
    below = lax.broadcasted_iota(jnp.int32, shape, 1) < lax.broadcasted_iota(jnp.int32, shape, 0)
    earlier = jnp.dot(
        below.astype(jnp.bfloat16),
        sum(onehots).astype(jnp.bfloat16),
        preferred_element_type=jnp.float32,
    )
    slot = lax.broadcasted_iota(jnp.int32, (row_count, experts * capacity), 1)
    spread = jnp.zeros(slot.shape, jnp.float32)
    for n, onehot in zip(named, onehots):
        place = jnp.sum(earlier * onehot, axis=1, keepdims=True).astype(jnp.int32)
        spread = spread + (slot == n * capacity + place).astype(jnp.float32)
    spread = spread.T.astype(jnp.bfloat16)
    piece = model_width // 7
    for lo in range(0, model_width, piece):
        columns = slice(lo, lo + piece)
        packed = jnp.dot(spread, rows[:, columns], preferred_element_type=jnp.float32)
        packed = packed.astype(jnp.bfloat16)
        outs[0][:, columns] = packed[: 2 * capacity]
        for i, out in enumerate(outs[1:]):
            out[:, columns] = packed[i * capacity : (i + 1) * capacity]


def pack(routes, rows, experts, capacity):
    counts = [2 * capacity] + [capacity] * experts
    return pl.pallas_call(
        functools.partial(pack_kernel, experts, capacity),
        out_shape=[jax.ShapeDtypeStruct((c, rows.shape[1]), jnp.bfloat16) for c in counts],
        compiler_params=pltpu.CompilerParams(vmem_limit_bytes=12 * 1024 * 1024),
        cost_estimate=pl.CostEstimate(
            flops=2 * rows.size * experts * capacity,
            bytes_accessed=2 * rows.size + 2 * sum(counts) * rows.shape[1],
            transcendentals=0,
        ),
    )(routes, rows)


def body(
    moe_rows,
    routes,
    gate_weights,
    gate_weight,
    up_weight,
    down_weight,
    queries,
    latent_cache,
    lengths,
):
    devices = lax.axis_size("ep")
    experts = devices // SPLIT
    outer_size = experts // 2
    row_count, model_width = moe_rows.shape
    top_count = routes.shape[1]
    capacity = 2 * row_count * top_count * SPLIT // devices
    me = lax.axis_index("ep")
    outer, inner = me // 8, me // 4 % 2

    def send(array, far=0, near=0, swap_x=0, swap_core=0):
        return lax.ppermute(array, "ep", permutation(devices, far, near, swap_x, swap_core))

    packed = pack(routes, moe_rows, experts, capacity)

    def outgoing_block(far, near):
        return packed[1 + far * 2 + near]

    close = sorted({1, outer_size - 1} - {0})
    rest = [(f, n) for f in range(2, outer_size - 1) for n in range(2)]
    near = [(close[0], n) for n in range(2)]
    last = [(close[1], n) for n in range(2)]
    rows, crossed = {(0, 0): outgoing_block(0, 0)}, {}

    def step(key, *first):
        rows[key] = send(after(outgoing_block(*key), *first), *key)

    def cross(keys, *first):
        together = jnp.concatenate([rows[key] for key in keys], axis=0)
        crossed[keys[0]] = send(after(together, *first) if first else together, swap_x=1)

    gate_other = send(gate_weight, swap_core=1)
    up_other = send(up_weight, swap_core=1)
    for key in rest:
        step(key)
    beside = send(packed[0], swap_x=1)
    begun = [gate_other, up_other, beside] + [rows[key] for key in rest]
    cross(rest, *begun)
    pair = jnp.concatenate([outgoing_block(0, 1), beside[capacity:]], axis=0)
    pair = send(after(pair, *begun), near=1)
    for key in near:
        step(key, *begun)
    down_other = send(after(down_weight, *begun), swap_core=1)
    begun = [crossed[rest[0]], down_other] + [rows[key] for key in near]
    for key in last:
        step(key, *begun)
    cross(near, *begun)

    mine, theirs = {}, {}

    def run(groups, returns, *others, resident=()):
        keys = [key for group in groups for key in group]
        blocks = [rows[key] for key in keys] + [crossed[group[0]] for group in groups]
        counts = (capacity,) * len(keys) + tuple(capacity * len(group) for group in returns)
        outs = expert(
            blocks + list(others),
            counts + tuple(other.shape[0] for other in others),
            (gate_weight, gate_other),
            (up_weight, up_other),
            (down_weight, down_other),
            resident,
        )
        mine.update(zip(keys, outs))
        theirs.update(zip([group[0] for group in returns], outs[len(keys) :]))
        return outs[len(counts) :]

    back, totals, returned = {}, {}, {}

    def give_back(keys, *first):
        back[keys[0]] = send(after(theirs[keys[0]], *first), swap_x=1)

    def add(one, other):
        return (one.astype(jnp.float32) + other.astype(jnp.float32)).astype(jnp.bfloat16)

    def finish(keys, *first):
        came = after(back[keys[0]], *first)
        for i, key in enumerate(keys):
            totals[key] = add(mine[key], came[i * capacity : (i + 1) * capacity])
            returned[key] = send(totals[key], -key[0], key[1])

    run([rest], [rest], resident=(0, 2))
    give_back(rest)
    cross(last, theirs[rest[0]])
    own_mine, own_theirs, own_pair = run(
        [near], [near], rows[0, 0], beside[:capacity], pair, resident=(0, 2)
    )
    give_back(near)
    finish(rest, mine[near[0]])
    own_pair = send(after(own_pair, *(totals[key] for key in rest)), near=1)
    singles = [[key] for key in last]
    run([last], singles)
    for keys in singles:
        give_back(keys, back[near[0]], *(returned[key] for key in rest))
    own_back = jnp.concatenate([own_theirs, own_pair[capacity:]], axis=0)
    own_back = send(after(own_back, back[last[0]]), swap_x=1)
    for keys in [near] + singles:
        finish(keys)
    own_back = after(own_back, returned[near[0]])
    returned[0, 0] = add(own_mine, own_back[:capacity])
    returned[0, 1] = add(own_pair[:capacity], own_back[capacity:])

    flat_routes = after(routes, theirs[near[0]]).reshape(-1)
    relative = (flat_routes // 2 - outer + outer_size) % outer_size * 2 + ((flat_routes % 2) ^ inner)
    onehot = (relative[:, None] == jnp.arange(experts, dtype=jnp.int32)[None, :]).astype(jnp.int32)
    earlier = jnp.cumsum(onehot, axis=0) - onehot
    slot_ids = jnp.sum(earlier * onehot, axis=1)
    targets = (relative * capacity + slot_ids).reshape(row_count, top_count)
    slots = jnp.arange(experts * capacity, dtype=jnp.int32)[None, None, :]
    places = targets[:, :, None] == slots
    places = places.astype(jnp.bfloat16).transpose(1, 0, 2)
    shares = after(gate_weights, theirs[near[0]])

    def gather(keys, dtype, *start):
        columns = [
            places[:, :, (f * 2 + n) * capacity : (f * 2 + n + 1) * capacity] for f, n in keys
        ]
        return combine(
            [returned[key] for key in keys],
            jnp.concatenate(columns, axis=2),
            shares,
            dtype,
            *start,
        )

    most = gather(rest + near, jnp.float32)
    moe_out = gather([(0, 0), (0, 1)] + last, jnp.bfloat16, most)
    attn_out = attention(after(queries, back[last[0]]), latent_cache, lengths)
    return (moe_out, attn_out)


def solution(mesh):
    in_specs = (
        P(("groups", "ep"), None),
        P(("groups", "ep"), None),
        P(("groups", "ep"), None),
        P(None, "ep"),
        P(None, "ep"),
        P("ep", None),
        P(("groups", "ep"), None, None),
        P(("groups", "ep"), None, None),
        P(("groups", "ep")),
    )
    out_specs = (P(("groups", "ep"), None), P(("groups", "ep"), None, None))
    return jax.shard_map(body, mesh=mesh, in_specs=in_specs, out_specs=out_specs, check_vma=False)
```

```python
import functools

import jax
import jax.numpy as jnp
from jax import lax
from jax.experimental import pallas as pl
from jax.experimental.pallas import tpu as pltpu
from jax.sharding import PartitionSpec as P

SPLIT = 4
NOPE = 512

softmax_scale = 192.0 ** (-0.5)


def attention(queries, latent_cache, lengths):
    scores = (
        jnp.einsum("rhc,rlc->rhl", queries, latent_cache, preferred_element_type=jnp.float32)
        * softmax_scale
    )
    positions = jnp.arange(latent_cache.shape[1], dtype=jnp.int32)
    valid_mask = positions[None, None, :] < lengths[:, None, None]
    scores = jnp.where(valid_mask, scores, -1e30)
    highest = jnp.max(scores, axis=-1, keepdims=True)
    expons = jnp.where(valid_mask, jnp.exp(scores - highest), 0.0)
    weights = (expons / jnp.sum(expons, axis=-1, keepdims=True)).astype(jnp.bfloat16)
    return jnp.einsum(
        "rhl,rlc->rhc", weights, latent_cache[:, :, :NOPE], preferred_element_type=jnp.float32
    ).astype(jnp.bfloat16)


def permutation(devices, far, near, swap_x, swap_core):
    outer_size = devices // 8
    pairs = []
    for source in range(devices):
        outer, inner, x, core = source // 8, source // 4 % 2, source // 2 % 2, source % 2
        target = ((outer + far) % outer_size * 2 + (inner ^ near)) * 4 + (x ^ swap_x) * 2 + (core ^ swap_core)
        pairs.append((source, target))
    return pairs


def after(array, *first):
    return lax.optimization_barrier((array,) + first)[0]


def expert_kernel(number, counts, parts, resident, *refs):
    blocks, weights, outs = refs[:number], refs[number : number + 6], refs[number + 6 : -5]
    wide, tall, total, hidden, arrived = refs[-5:]
    model_width, width = weights[0].shape
    part_width = model_width // parts
    spans = [slice(p * part_width, (p + 1) * part_width) for p in range(parts)]
    fetched = [i for i in range(4) if i not in resident]
    wide_copies = [
        {
            i: pltpu.make_async_copy(
                weights[i].at[span], wide.at[at, span], arrived.at[p * 6 + at]
            )
            for at, i in enumerate(fetched)
        }
        for p, span in enumerate(spans)
    ]
    tall_copies = [
        [
            pltpu.make_async_copy(
                weights[4 + i].at[:, span], tall.at[i, :, span], arrived.at[p * 6 + 4 + i]
            )
            for i in range(2)
        ]
        for p, span in enumerate(spans)
    ]
    for copies in [list(c.values()) for c in wide_copies] + tall_copies:
        for copy in copies:
            copy.start()
    order = [(p, i) for p in range(parts) for i in resident]
    order += [(p, i) for p in range(parts) for i in fetched]
    for p, i in order:
        span = spans[p]
        rows = jnp.concatenate([b[:, span] for b in blocks], axis=0)
        if i in resident:
            weight = weights[i][span]
        else:
            wide_copies[p][i].wait()
            weight = wide[fetched.index(i), span]
        product = jnp.dot(rows, weight, preferred_element_type=jnp.float32)
        columns = slice(i * width, (i + 1) * width)
        total[:, columns] = product if p == 0 else total[:, columns] + product
    gate, up = total[:, : 2 * width], total[:, 2 * width :]
    hidden[...] = (gate / (1.0 + jnp.exp(-gate)) * up).astype(jnp.bfloat16)
    piece = part_width // 4
    for p in range(parts):
        for copy in tall_copies[p]:
            copy.wait()
        for q in range(4):
            columns = slice(p * part_width + q * piece, p * part_width + (q + 1) * piece)
            part = jnp.dot(
                hidden[:, :width], tall[0, :, columns], preferred_element_type=jnp.float32
            )
            part += jnp.dot(
                hidden[:, width:], tall[1, :, columns], preferred_element_type=jnp.float32
            )
            part = part.astype(jnp.bfloat16)
            at = 0
            for count, out in zip(counts, outs):
                out[:, columns] = part[at : at + count]
                at += count


def expert(blocks, counts, gates, ups, downs, resident=()):
    model_width, width = gates[0].shape
    slots, parts = sum(counts), 2
    return pl.pallas_call(
        functools.partial(expert_kernel, len(blocks), counts, parts, resident),
        in_specs=[pl.BlockSpec(memory_space=pltpu.VMEM)] * len(blocks)
        + [
            pl.BlockSpec(memory_space=pltpu.VMEM if i in resident else pl.ANY) for i in range(6)
        ],
        out_specs=[pl.BlockSpec(memory_space=pltpu.VMEM)] * len(counts),
        out_shape=[jax.ShapeDtypeStruct((c, model_width), jnp.bfloat16) for c in counts],
        scratch_shapes=[
            pltpu.VMEM((4 - len(resident), model_width, width), jnp.bfloat16),
            pltpu.VMEM((2, width, model_width), jnp.bfloat16),
            pltpu.VMEM((slots, 4 * width), jnp.float32),
            pltpu.VMEM((slots, 2 * width), jnp.bfloat16),
            pltpu.SemaphoreType.DMA((6 * parts,)),
        ],
        compiler_params=pltpu.CompilerParams(vmem_limit_bytes=(40 if resident else 60) * 1024 * 1024),
        cost_estimate=pl.CostEstimate(
            flops=12 * slots * model_width * width,
            bytes_accessed=12 * model_width * width + 4 * slots * model_width,
            transcendentals=2 * slots * width,
        ),
    )(*blocks, *gates, *ups, *downs)


def combine_kernel(number, start, *refs):
    blocks, (places, shares), out = refs[:number], refs[number : number + 2], refs[-1]
    model_width = out.shape[1]
    piece = model_width // 7
    for lo in range(0, model_width, piece):
        columns = slice(lo, lo + piece)
        rows = jnp.concatenate([b[:, columns] for b in blocks], axis=0)
        total = refs[number + 2][:, columns] if start else 0.0
        for k in range(shares.shape[1]):
            picked = jnp.dot(places[k], rows, preferred_element_type=jnp.float32)
            total = total + picked * shares[:, k : k + 1]
        out[:, columns] = total.astype(out.dtype)


def combine(blocks, places, shares, dtype, *start):
    return pl.pallas_call(
        functools.partial(combine_kernel, len(blocks), bool(start)),
        out_shape=jax.ShapeDtypeStruct((shares.shape[0], blocks[0].shape[1]), dtype),
    )(*blocks, places, shares, *start)


def body(
    moe_rows,
    routes,
    gate_weights,
    gate_weight,
    up_weight,
    down_weight,
    queries,
    latent_cache,
    lengths,
):
    devices = lax.axis_size("ep")
    experts = devices // SPLIT
    outer_size = experts // 2
    row_count, model_width = moe_rows.shape
    top_count = routes.shape[1]
    capacity = 2 * row_count * top_count * SPLIT // devices
    me = lax.axis_index("ep")
    outer, inner = me // 8, me // 4 % 2

    def send(array, far=0, near=0, swap_x=0, swap_core=0):
        return lax.ppermute(array, "ep", permutation(devices, far, near, swap_x, swap_core))

    flat_routes = routes.reshape(-1)
    relative = (flat_routes // 2 - outer + outer_size) % outer_size * 2 + ((flat_routes % 2) ^ inner)
    onehot = (relative[:, None] == jnp.arange(experts, dtype=jnp.int32)[None, :]).astype(jnp.int32)
    earlier = jnp.cumsum(onehot, axis=0) - onehot
    slot_ids = jnp.sum(earlier * onehot, axis=1)
    targets = (relative * capacity + slot_ids).reshape(row_count, top_count)
    slots = jnp.arange(experts * capacity, dtype=jnp.int32)[None, None, :]
    spread = jnp.any(targets[:, :, None] == slots, axis=1).astype(jnp.bfloat16)
    outgoing = jnp.einsum(
        "rp,rd->pd", spread, moe_rows, preferred_element_type=jnp.float32
    ).astype(jnp.bfloat16)

    def outgoing_block(far, near):
        at = (far * 2 + near) * capacity
        return outgoing[at : at + capacity]

    close = sorted({1, outer_size - 1} - {0})
    rest = [(f, n) for f in range(2, outer_size - 1) for n in range(2)]
    near = [(close[0], n) for n in range(2)]
    last = [(close[1], n) for n in range(2)]
    rows, crossed = {(0, 0): outgoing_block(0, 0)}, {}

    def step(key, *first):
        rows[key] = send(after(outgoing_block(*key), *first), *key)

    def cross(keys, *first):
        together = jnp.concatenate([rows[key] for key in keys], axis=0)
        crossed[keys[0]] = send(after(together, *first) if first else together, swap_x=1)

    gate_other = send(gate_weight, swap_core=1)
    up_other = send(up_weight, swap_core=1)
    for key in rest:
        step(key)
    beside = send(outgoing[: 2 * capacity], swap_x=1)
    begun = [gate_other, up_other, beside] + [rows[key] for key in rest]
    cross(rest, *begun)
    pair = jnp.concatenate([outgoing_block(0, 1), beside[capacity:]], axis=0)
    pair = send(after(pair, *begun), near=1)
    for key in near:
        step(key, *begun)
    down_other = send(after(down_weight, *begun), swap_core=1)
    begun = [crossed[rest[0]], down_other] + [rows[key] for key in near]
    cross(near)
    for key in last:
        step(key, *begun)

    mine, theirs = {}, {}

    def run(groups, returns, *others, resident=()):
        keys = [key for group in groups for key in group]
        blocks = [rows[key] for key in keys] + [crossed[group[0]] for group in groups]
        counts = (capacity,) * len(keys) + tuple(capacity * len(group) for group in returns)
        outs = expert(
            blocks + list(others),
            counts + tuple(other.shape[0] for other in others),
            (gate_weight, gate_other),
            (up_weight, up_other),
            (down_weight, down_other),
            resident,
        )
        mine.update(zip(keys, outs))
        theirs.update(zip([group[0] for group in returns], outs[len(keys) :]))
        return outs[len(counts) :]

    back, totals, returned = {}, {}, {}

    def give_back(keys, *first):
        back[keys[0]] = send(after(theirs[keys[0]], *first), swap_x=1)

    def add(one, other):
        return (one.astype(jnp.float32) + other.astype(jnp.float32)).astype(jnp.bfloat16)

    def finish(keys, *first):
        came = after(back[keys[0]], *first)
        for i, key in enumerate(keys):
            totals[key] = add(mine[key], came[i * capacity : (i + 1) * capacity])
            returned[key] = send(totals[key], -key[0], key[1])

    run([rest], [rest], resident=(0, 2))
    give_back(rest)
    cross(last, theirs[rest[0]])
    own_mine, own_theirs, own_pair = run(
        [near], [near], after(rows[0, 0], rows[last[-1]]), beside[:capacity], pair, resident=(0, 2)
    )
    give_back(near)
    finish(rest, mine[near[0]])
    own_pair = send(after(own_pair, *(totals[key] for key in rest)), near=1)
    singles = [[key] for key in last]
    run([last], singles)
    for keys in singles:
        give_back(keys, back[near[0]], *(returned[key] for key in rest))
    own_back = jnp.concatenate([own_theirs, own_pair[capacity:]], axis=0)
    own_back = send(after(own_back, back[last[0]]), swap_x=1)
    for keys in [near] + singles:
        finish(keys)
    own_back = after(own_back, returned[near[0]])
    returned[0, 0] = add(own_mine, own_back[:capacity])
    returned[0, 1] = add(own_pair[:capacity], own_back[capacity:])

    places = after(targets, theirs[near[0]])[:, :, None] == slots
    places = places.astype(jnp.bfloat16).transpose(1, 0, 2)
    shares = after(gate_weights, theirs[near[0]])

    def gather(keys, dtype, *start):
        columns = [
            places[:, :, (f * 2 + n) * capacity : (f * 2 + n + 1) * capacity] for f, n in keys
        ]
        return combine(
            [returned[key] for key in keys],
            jnp.concatenate(columns, axis=2),
            shares,
            dtype,
            *start,
        )

    most = gather(rest + near, jnp.float32)
    moe_out = gather([(0, 0), (0, 1)] + last, jnp.bfloat16, most)
    attn_out = attention(after(queries, back[last[0]]), latent_cache, lengths)
    return (moe_out, attn_out)


def solution(mesh):
    in_specs = (
        P(("groups", "ep"), None),
        P(("groups", "ep"), None),
        P(("groups", "ep"), None),
        P(None, "ep"),
        P(None, "ep"),
        P("ep", None),
        P(("groups", "ep"), None, None),
        P(("groups", "ep"), None, None),
        P(("groups", "ep")),
    )
    out_specs = (P(("groups", "ep"), None), P(("groups", "ep"), None, None))
    return jax.shard_map(body, mesh=mesh, in_specs=in_specs, out_specs=out_specs, check_vma=False)
```

```python
import functools

import jax
import jax.numpy as jnp
from jax import lax
from jax.experimental import pallas as pl
from jax.experimental.pallas import tpu as pltpu
from jax.sharding import PartitionSpec as P

SPLIT = 4
NOPE = 512

softmax_scale = 192.0 ** (-0.5)


def attention(queries, latent_cache, lengths):
    scores = (
        jnp.einsum("rhc,rlc->rhl", queries, latent_cache, preferred_element_type=jnp.float32)
        * softmax_scale
    )
    positions = jnp.arange(latent_cache.shape[1], dtype=jnp.int32)
    valid_mask = positions[None, None, :] < lengths[:, None, None]
    scores = jnp.where(valid_mask, scores, -1e30)
    highest = jnp.max(scores, axis=-1, keepdims=True)
    expons = jnp.where(valid_mask, jnp.exp(scores - highest), 0.0)
    weights = (expons / jnp.sum(expons, axis=-1, keepdims=True)).astype(jnp.bfloat16)
    return jnp.einsum(
        "rhl,rlc->rhc", weights, latent_cache[:, :, :NOPE], preferred_element_type=jnp.float32
    ).astype(jnp.bfloat16)


def permutation(devices, far, near, swap_x, swap_core):
    outer_size = devices // 8
    pairs = []
    for source in range(devices):
        outer, inner, x, core = source // 8, source // 4 % 2, source // 2 % 2, source % 2
        target = ((outer + far) % outer_size * 2 + (inner ^ near)) * 4 + (x ^ swap_x) * 2 + (core ^ swap_core)
        pairs.append((source, target))
    return pairs


def after(array, *first):
    return lax.optimization_barrier((array,) + first)[0]


def expert_kernel(number, counts, parts, resident, *refs):
    blocks, weights, outs = refs[:number], refs[number : number + 6], refs[number + 6 : -5]
    wide, tall, total, hidden, arrived = refs[-5:]
    model_width, width = weights[0].shape
    part_width = model_width // parts
    spans = [slice(p * part_width, (p + 1) * part_width) for p in range(parts)]
    fetched = [i for i in range(4) if i not in resident]
    wide_copies = [
        {
            i: pltpu.make_async_copy(
                weights[i].at[span], wide.at[at, span], arrived.at[p * 6 + at]
            )
            for at, i in enumerate(fetched)
        }
        for p, span in enumerate(spans)
    ]
    tall_copies = [
        [
            pltpu.make_async_copy(
                weights[4 + i].at[:, span], tall.at[i, :, span], arrived.at[p * 6 + 4 + i]
            )
            for i in range(2)
        ]
        for p, span in enumerate(spans)
    ]
    for copies in [list(c.values()) for c in wide_copies] + tall_copies:
        for copy in copies:
            copy.start()
    order = [(p, i) for p in range(parts) for i in resident]
    order += [(p, i) for p in range(parts) for i in fetched]
    for p, i in order:
        span = spans[p]
        rows = jnp.concatenate([b[:, span] for b in blocks], axis=0)
        if i in resident:
            weight = weights[i][span]
        else:
            wide_copies[p][i].wait()
            weight = wide[fetched.index(i), span]
        product = jnp.dot(rows, weight, preferred_element_type=jnp.float32)
        columns = slice(i * width, (i + 1) * width)
        total[:, columns] = product if p == 0 else total[:, columns] + product
    gate, up = total[:, : 2 * width], total[:, 2 * width :]
    hidden[...] = (gate / (1.0 + jnp.exp(-gate)) * up).astype(jnp.bfloat16)
    piece = part_width // 4
    for p in range(parts):
        for copy in tall_copies[p]:
            copy.wait()
        for q in range(4):
            columns = slice(p * part_width + q * piece, p * part_width + (q + 1) * piece)
            part = jnp.dot(
                hidden[:, :width], tall[0, :, columns], preferred_element_type=jnp.float32
            )
            part += jnp.dot(
                hidden[:, width:], tall[1, :, columns], preferred_element_type=jnp.float32
            )
            part = part.astype(jnp.bfloat16)
            at = 0
            for count, out in zip(counts, outs):
                out[:, columns] = part[at : at + count]
                at += count


def expert(blocks, counts, gates, ups, downs, resident=()):
    model_width, width = gates[0].shape
    slots, parts = sum(counts), 2
    return pl.pallas_call(
        functools.partial(expert_kernel, len(blocks), counts, parts, resident),
        in_specs=[pl.BlockSpec(memory_space=pltpu.VMEM)] * len(blocks)
        + [
            pl.BlockSpec(memory_space=pltpu.VMEM if i in resident else pl.ANY) for i in range(6)
        ],
        out_specs=[pl.BlockSpec(memory_space=pltpu.VMEM)] * len(counts),
        out_shape=[jax.ShapeDtypeStruct((c, model_width), jnp.bfloat16) for c in counts],
        scratch_shapes=[
            pltpu.VMEM((4 - len(resident), model_width, width), jnp.bfloat16),
            pltpu.VMEM((2, width, model_width), jnp.bfloat16),
            pltpu.VMEM((slots, 4 * width), jnp.float32),
            pltpu.VMEM((slots, 2 * width), jnp.bfloat16),
            pltpu.SemaphoreType.DMA((6 * parts,)),
        ],
        compiler_params=pltpu.CompilerParams(vmem_limit_bytes=(40 if resident else 60) * 1024 * 1024),
        cost_estimate=pl.CostEstimate(
            flops=12 * slots * model_width * width,
            bytes_accessed=12 * model_width * width + 4 * slots * model_width,
            transcendentals=2 * slots * width,
        ),
    )(*blocks, *gates, *ups, *downs)


def combine_kernel(number, start, *refs):
    blocks, (places, shares), out = refs[:number], refs[number : number + 2], refs[-1]
    model_width = out.shape[1]
    piece = model_width // 4
    for lo in range(0, model_width, piece):
        columns = slice(lo, lo + piece)
        rows = jnp.concatenate([b[:, columns] for b in blocks], axis=0)
        total = refs[number + 2][:, columns] if start else 0.0
        for k in range(shares.shape[1]):
            picked = jnp.dot(places[k], rows, preferred_element_type=jnp.float32)
            total = total + picked * shares[:, k : k + 1]
        out[:, columns] = total.astype(out.dtype)


def combine(blocks, places, shares, dtype, *start):
    return pl.pallas_call(
        functools.partial(combine_kernel, len(blocks), bool(start)),
        out_shape=jax.ShapeDtypeStruct((shares.shape[0], blocks[0].shape[1]), dtype),
    )(*blocks, places, shares, *start)


def body(
    moe_rows,
    routes,
    gate_weights,
    gate_weight,
    up_weight,
    down_weight,
    queries,
    latent_cache,
    lengths,
):
    devices = lax.axis_size("ep")
    experts = devices // SPLIT
    outer_size = experts // 2
    row_count, model_width = moe_rows.shape
    top_count = routes.shape[1]
    capacity = 2 * row_count * top_count * SPLIT // devices
    me = lax.axis_index("ep")
    outer, inner = me // 8, me // 4 % 2

    def send(array, far=0, near=0, swap_x=0, swap_core=0):
        return lax.ppermute(array, "ep", permutation(devices, far, near, swap_x, swap_core))

    flat_routes = routes.reshape(-1)
    relative = (flat_routes // 2 - outer + outer_size) % outer_size * 2 + ((flat_routes % 2) ^ inner)
    onehot = (relative[:, None] == jnp.arange(experts, dtype=jnp.int32)[None, :]).astype(jnp.int32)
    earlier = jnp.cumsum(onehot, axis=0) - onehot
    slot_ids = jnp.sum(earlier * onehot, axis=1)
    targets = (relative * capacity + slot_ids).reshape(row_count, top_count)
    slots = jnp.arange(experts * capacity, dtype=jnp.int32)[None, None, :]
    spread = jnp.any(targets[:, :, None] == slots, axis=1).astype(jnp.bfloat16)
    outgoing = jnp.einsum(
        "rp,rd->pd", spread, moe_rows, preferred_element_type=jnp.float32
    ).astype(jnp.bfloat16)

    def outgoing_block(far, near):
        at = (far * 2 + near) * capacity
        return outgoing[at : at + capacity]

    close = sorted({1, outer_size - 1} - {0})
    rest = [(f, n) for f in range(2, outer_size - 1) for n in range(2)]
    near = [(close[0], n) for n in range(2)]
    last = [(close[1], n) for n in range(2)]
    rows, crossed = {(0, 0): outgoing_block(0, 0)}, {}

    def step(key, *first):
        rows[key] = send(after(outgoing_block(*key), *first), *key)

    def cross(keys, *first):
        together = jnp.concatenate([rows[key] for key in keys], axis=0)
        crossed[keys[0]] = send(after(together, *first) if first else together, swap_x=1)

    gate_other = send(gate_weight, swap_core=1)
    up_other = send(up_weight, swap_core=1)
    for key in rest:
        step(key)
    beside = send(outgoing[: 2 * capacity], swap_x=1)
    begun = [gate_other, up_other, beside] + [rows[key] for key in rest]
    cross(rest, *begun)
    pair = jnp.concatenate([outgoing_block(0, 1), beside[capacity:]], axis=0)
    pair = send(after(pair, *begun), near=1)
    for key in near:
        step(key, *begun)
    down_other = send(after(down_weight, *begun), swap_core=1)
    begun = [crossed[rest[0]], down_other] + [rows[key] for key in near]
    for key in last:
        step(key, *begun)
    cross(near, *begun)

    mine, theirs = {}, {}

    def run(groups, returns, *others, resident=()):
        keys = [key for group in groups for key in group]
        blocks = [rows[key] for key in keys] + [crossed[group[0]] for group in groups]
        counts = (capacity,) * len(keys) + tuple(capacity * len(group) for group in returns)
        outs = expert(
            blocks + list(others),
            counts + tuple(other.shape[0] for other in others),
            (gate_weight, gate_other),
            (up_weight, up_other),
            (down_weight, down_other),
            resident,
        )
        mine.update(zip(keys, outs))
        theirs.update(zip([group[0] for group in returns], outs[len(keys) :]))
        return outs[len(counts) :]

    back, totals, returned = {}, {}, {}

    def give_back(keys, *first):
        back[keys[0]] = send(after(theirs[keys[0]], *first), swap_x=1)

    def add(one, other):
        return (one.astype(jnp.float32) + other.astype(jnp.float32)).astype(jnp.bfloat16)

    def finish(keys, *first):
        came = after(back[keys[0]], *first)
        for i, key in enumerate(keys):
            totals[key] = add(mine[key], came[i * capacity : (i + 1) * capacity])
            returned[key] = send(totals[key], -key[0], key[1])

    run([rest], [rest], resident=(0, 2))
    give_back(rest)
    cross(last, theirs[rest[0]])
    own_mine, own_theirs, own_pair = run(
        [near], [near], rows[0, 0], beside[:capacity], pair, resident=(0, 2)
    )
    give_back(near)
    finish(rest, mine[near[0]])
    own_pair = send(after(own_pair, *(totals[key] for key in rest)), near=1)
    singles = [[key] for key in last]
    run([last], singles)
    for keys in singles:
        give_back(keys, back[near[0]], *(returned[key] for key in rest))
    own_back = jnp.concatenate([own_theirs, own_pair[capacity:]], axis=0)
    own_back = send(after(own_back, back[last[0]]), swap_x=1)
    for keys in [near] + singles:
        finish(keys)
    own_back = after(own_back, returned[near[0]])
    returned[0, 0] = add(own_mine, own_back[:capacity])
    returned[0, 1] = add(own_pair[:capacity], own_back[capacity:])

    places = after(targets, theirs[near[0]])[:, :, None] == slots
    places = places.astype(jnp.bfloat16).transpose(1, 0, 2)
    shares = after(gate_weights, theirs[near[0]])

    def gather(keys, dtype, *start):
        columns = [
            places[:, :, (f * 2 + n) * capacity : (f * 2 + n + 1) * capacity] for f, n in keys
        ]
        return combine(
            [returned[key] for key in keys],
            jnp.concatenate(columns, axis=2),
            shares,
            dtype,
            *start,
        )

    most = gather(rest + near, jnp.float32)
    moe_out = gather([(0, 0), (0, 1)] + last, jnp.bfloat16, most)
    attn_out = attention(after(queries, back[last[0]]), latent_cache, lengths)
    return (moe_out, attn_out)


def solution(mesh):
    in_specs = (
        P(("groups", "ep"), None),
        P(("groups", "ep"), None),
        P(("groups", "ep"), None),
        P(None, "ep"),
        P(None, "ep"),
        P("ep", None),
        P(("groups", "ep"), None, None),
        P(("groups", "ep"), None, None),
        P(("groups", "ep")),
    )
    out_specs = (P(("groups", "ep"), None), P(("groups", "ep"), None, None))
    return jax.shard_map(body, mesh=mesh, in_specs=in_specs, out_specs=out_specs, check_vma=False)
```
